256 devices in a mesh: ctx: 32 (over x_lo, z, core), head: 8 (over y, x_hi).
Axes of the slice: x: 4 (x_hi: 2, x_lo: 2; x = x_hi * 2 + x_lo), y: 4, z: 8, core: 2. Of those that a mesh axis runs over, the one named last changes fastest.
Arguments:
- q_latent: bfloat16 [4096, 1536], P(('ctx', 'head')), may hold values from -320 to 320
- q_gain: float32 [1536], replicated, may hold values from 0.5 to 8
- kv_cache: bfloat16 [4096, 576], P(('ctx', 'head')), may hold values from -320 to 320
- kv_gain: float32 [512], replicated, may hold values from 0.5 to 8
- w_query: bfloat16 [1536, 12288], P(None, 'head'), may hold values from -0.15625 to 0.15625
- w_kv: bfloat16 [512, 16384], P(None, 'head'), may hold values from -0.25 to 0.25
- doc_lengths: int32 [3], replicated, may hold values from 1 to 2048, 4096 in all
Outputs:
- attn_out: bfloat16 [4096, 8192], P('ctx', 'head')
The draws below stay inside these ranges and needn't reach their ends.
Inputs may be any that keep to these rules, and one draw needn't show every extreme that they name: `doc_lengths`: 3 documents, lengths in order summing to 4096; the longest has exactly 2048 tokens.
All inputs are finite; a program needn't handle non-finite values.
Results may differ from the reference program's by a relative error of at most 0.0075.
The reference program's roundings to bfloat16 on the way count: a program that leaves them out, or rounds other values in their place, can miss the bound.
Values may be sent and summed in bfloat16 or wider, within the bound.
No kernel may reach another device: no remote copies, remote signals or barrier semaphores. Data moves between devices by JAX's collectives and lax.ppermute only.
A program may use at most 192 MiB of HBM per device.

```python
import math
import jax
import jax.numpy as jnp
import numpy as np
from jax import lax

QL = 1536
KL = 512
RD = 64
ND = 128
VD = 128
HEADS = 64
DOCS = 3
SEQ = 4096


def scaled_rows(key, row_count, col_count, plain_cols):
    normal_key = jax.random.fold_in(key, 101)
    row_key = jax.random.fold_in(key, 202)
    col_key = jax.random.fold_in(key, 303)
    values = jax.random.truncated_normal(normal_key, -4.0, 4.0, (row_count, col_count), jnp.float32)
    row_top = math.log(10.0)
    row_scale = jnp.exp(jax.random.uniform(row_key, (row_count, 1), jnp.float32, 0.0, row_top))
    col_scale = jnp.exp(jax.random.uniform(col_key, (1, col_count), jnp.float32, 0.0, math.log(3.0)))
    column_index = jnp.arange(col_count, dtype=jnp.int32)[None, :]
    scaled = values * row_scale * col_scale
    return jnp.where(column_index < col_count - plain_cols, scaled, values)


def gain_values(key, width):
    return jax.random.uniform(key, (width,), jnp.float32, 0.5, 1.5)


def draw_q_latent(key, part):
    return scaled_rows(jax.random.fold_in(key, 11), SEQ, QL, 0).astype(jnp.bfloat16)


def draw_kv_cache(key, part):
    return scaled_rows(jax.random.fold_in(key, 23), SEQ, KL + RD, RD).astype(jnp.bfloat16)


def draw_q_gain(key, part):
    return gain_values(jax.random.fold_in(key, 37), QL)


def draw_kv_gain(key, part):
    return gain_values(jax.random.fold_in(key, 41), KL)


def block_levels(own_key, dims, pieces, smallest, high):
    factor_of = 1.0
    for axis_at, shards_of in pieces:
        draws = jax.random.uniform(jax.random.fold_in(jax.random.fold_in(own_key, 6), axis_at), (shards_of,), jnp.float32, smallest / len(pieces), high / len(pieces))
        factor_of = factor_of * jnp.repeat(jnp.exp(draws), dims[axis_at] // shards_of).reshape((-1,) + (1,) * (len(dims) - 1 - axis_at))
    return factor_of


def split_up(count, total, most, slope):
    loads = [(1 << 20) // math.isqrt(grade ** slope) + 1 for grade in range(2, count + 1)]
    surplus, holding = total - most - (count - 1), [1] * (count - 1)
    while surplus > 0:
        movable = [i for i in range(count - 1) if holding[i] < most]
        whole, budget = sum([loads[i] for i in movable]), surplus
        for i in movable:
            more = min(most - holding[i], max(1, budget * loads[i] // whole), surplus)
            holding[i] = holding[i] + more
            surplus = surplus - more
    return np.array([most] + holding)


def ragged(own_key, count, total, reach, slope):
    if count == 2:
        one = jax.random.randint(own_key, (), max(1, total - reach), min(reach, total - 1) + 1)
        return jnp.stack([one, total - one])
    sizes = jnp.asarray(split_up(count, total, reach, slope), jnp.int32)
    pairs = (count - 1) // 2
    source_of, receiver = sizes[1:1 + 2 * pairs:2], sizes[2:2 + 2 * pairs:2]
    slack = jnp.minimum(source_of - 1, reach - receiver)
    moved = jax.random.randint(jax.random.fold_in(own_key, 1), (pairs,), 0, 1 << 20) % (slack + 1)
    sizes = sizes.at[1:1 + 2 * pairs:2].set(source_of - moved).at[2:2 + 2 * pairs:2].set(receiver + moved)
    return sizes[jax.random.permutation(jax.random.fold_in(own_key, 2), count)]


def normal_values(own_key, dims, scale, reach, pieces=(), kind=jnp.bfloat16):
    level = block_levels(own_key, dims, pieces, -0.22, 0.18) if pieces else 1.0
    entries = jax.random.normal(own_key, dims, jnp.float32) * scale * level
    return jnp.minimum(jnp.maximum(entries, -reach), reach).astype(kind)


def setup_inputs(seed: int = 0) -> dict:
    streams_of = jax.random.split(jax.random.key(seed), 8)
    return {
        "q_latent": draw_q_latent(jax.random.fold_in(streams_of[7], 71), 0),
        "q_gain": draw_q_gain(jax.random.fold_in(streams_of[7], 71), 0),
        "kv_cache": draw_kv_cache(jax.random.fold_in(streams_of[7], 71), 0),
        "kv_gain": draw_kv_gain(jax.random.fold_in(streams_of[7], 71), 0),
        "w_query": normal_values(streams_of[4], (QL, HEADS * (ND + RD)), QL ** -0.5, 0.15625, ((1, 8),)),
        "w_kv": normal_values(streams_of[5], (KL, HEADS * (ND + VD)), KL ** -0.5, 0.25, ((1, 8),)),
        "doc_lengths": ragged(streams_of[6], DOCS, SEQ, SEQ // 2, 0).astype(jnp.int32),
    }


epsilon = 1e-06

def rms_scale(rows, gain):
    values = rows.astype(jnp.float32)
    return values * lax.rsqrt(lax.optimization_barrier(jnp.mean(values * values, axis=-1, keepdims=True)) + epsilon) * gain

def doc_tables(doc_lengths, positions):
    doc_ends = jnp.cumsum(doc_lengths).astype(jnp.int32)
    passed = positions[:, None] >= doc_ends[None, :]
    doc_index = lax.optimization_barrier(jnp.sum(passed.astype(jnp.int32), axis=1)).astype(jnp.int32)
    doc_start = lax.optimization_barrier(jnp.sum(jnp.where(passed, doc_lengths[None, :], 0), axis=1)).astype(jnp.int32)
    return (doc_index, doc_start)

def rotate_pairs(values, offsets):
    half_width = values.shape[-1] // 2
    freq_index = jnp.arange(half_width, dtype=jnp.float32)
    frequency = jnp.exp(freq_index * (-2.0 * math.log(10000.0) / values.shape[-1]))
    angles = offsets.astype(jnp.float32)[:, None] * frequency[None, :]
    cosine = jnp.cos(angles)[:, None, :]
    sine_part = jnp.sin(angles)[:, None, :]
    lower_half = values[..., :half_width]
    upper_half = values[..., half_width:]
    return jnp.concatenate([lower_half * cosine - upper_half * sine_part, upper_half * cosine + lower_half * sine_part], axis=-1)

def project_queries(latent_rows, q_gain, w_query, offsets, nope_width, rope_width):
    normed = rms_scale(latent_rows, q_gain).astype(jnp.bfloat16)
    projected = jnp.dot(normed, w_query, preferred_element_type=jnp.float32)
    head_count = w_query.shape[1] // (nope_width + rope_width)
    projected = projected.reshape(latent_rows.shape[0], head_count, nope_width + rope_width)
    rotated = rotate_pairs(projected[..., nope_width:], offsets)
    return jnp.concatenate([projected[..., :nope_width], rotated], axis=-1).astype(jnp.bfloat16)

def reference(q_latent, q_gain, kv_cache, kv_gain, w_query, w_kv, doc_lengths):
    positions = jnp.arange(SEQ, dtype=jnp.int32)
    doc_index, doc_start = doc_tables(doc_lengths, positions)
    queries = project_queries(q_latent, q_gain, w_query, positions - doc_start, ND, RD)
    kv_normed = rms_scale(kv_cache[:, :KL], kv_gain).astype(jnp.bfloat16)
    expanded = jnp.dot(kv_normed, w_kv, preferred_element_type=jnp.float32).astype(jnp.bfloat16)
    expanded = expanded.reshape(SEQ, HEADS, ND + VD)
    key_rope = kv_cache[:, KL:]
    block_size = min(512, SEQ)
    window = min(SEQ, SEQ // 2 + block_size)
    score_scale = 1.0 / math.sqrt(ND + RD)

    def one_block(number):
        first_row = (number * block_size).astype(jnp.int32)
        key_first = jnp.clip(first_row + block_size - window, 0, SEQ - window).astype(jnp.int32)
        query_block = lax.dynamic_slice_in_dim(queries, first_row, block_size, 0).astype(jnp.float32)
        key_block = lax.dynamic_slice_in_dim(expanded, key_first, window, 0).astype(jnp.float32)
        rope_block = lax.dynamic_slice_in_dim(key_rope, key_first, window, 0).astype(jnp.float32)
        scores = jnp.einsum('qhd,khd->hqk', query_block[..., :ND], key_block[..., :ND])
        scores = (scores + jnp.einsum('qhr,kr->hqk', query_block[..., ND:], rope_block)) * score_scale
        query_pos = first_row + jnp.arange(block_size, dtype=jnp.int32)
        key_pos = key_first + jnp.arange(window, dtype=jnp.int32)
        query_doc = lax.dynamic_slice_in_dim(doc_index, first_row, block_size, 0)
        key_doc = lax.dynamic_slice_in_dim(doc_index, key_first, window, 0)
        allowed = (key_pos[None, :] <= query_pos[:, None]) & (key_doc[None, :] == query_doc[:, None])
        masked = jnp.where(allowed[None], scores, -1e+30)
        running_max = lax.optimization_barrier(jnp.max(masked, axis=-1))
        weights = jnp.where(allowed[None], jnp.exp(scores - running_max[..., None]), 0.0)
        row_total = lax.optimization_barrier(jnp.sum(weights, axis=-1))
        rounded = lax.optimization_barrier(weights.astype(jnp.bfloat16))
        mixed = jnp.einsum('hqk,khv->qhv', rounded.astype(jnp.float32), key_block[..., ND:])
        mixed = mixed / jnp.transpose(row_total)[:, :, None]
        return mixed.reshape(block_size, HEADS * VD)
    outputs = lax.map(one_block, jnp.arange(SEQ // block_size, dtype=jnp.int32))
    return outputs.reshape(SEQ, HEADS * VD).astype(jnp.bfloat16)
```

```python
import math

import jax
import jax.numpy as jnp
import numpy as np
from jax import lax
from jax.experimental import pallas as pl
from jax.experimental.pallas import tpu as pltpu
from jax.sharding import PartitionSpec as P

KL = 512
RD = 64
ND = 128
VD = 128
LANES = 128
EPSILON = 1e-06
MASKED = -1e30
FLOOR = -1e29
SCORE_SCALE = math.log2(math.e) / math.sqrt(ND + RD)


def norm_kernel(q_ref, qg_ref, kv_ref, kg_ref, q_out, kv_out):
    def scaled(values, gain):
        mean = jnp.mean(values * values, axis=-1, keepdims=True)
        return values * lax.rsqrt(mean + EPSILON) * gain

    q_out[...] = scaled(q_ref[...].astype(jnp.float32), qg_ref[...]).astype(jnp.bfloat16)
    latent = kv_ref[:, :KL].astype(jnp.float32)
    kv_out[:, :KL] = scaled(latent, kg_ref[...]).astype(jnp.bfloat16)
    kv_out[:, KL:] = kv_ref[:, KL:]


def query_kernel(places, own, after, before, across, cos_ref, sin_ref, w_ref, out_ref, rows_ref):
    @pl.when(pl.program_id(0) == 0)
    def _():
        for n, ref in enumerate((own, after, before, across)):
            for half in range(2):
                at = pl.multiple_of(places[2 * n + half], 16)
                rows_ref[pl.ds(at, 16), :] = ref[16 * half : 16 * half + 16, :]

    made = jnp.dot(rows_ref[...], w_ref[...], preferred_element_type=jnp.float32)
    lane = lax.broadcasted_iota(jnp.int32, (made.shape[0], LANES), 1)

    def rotated(rope):
        turned = jnp.where(
            lane < RD // 2, pltpu.roll(rope, LANES - RD // 2, 1), pltpu.roll(rope, RD // 2, 1)
        )
        return rope * cos_ref[...] + turned * sin_ref[...]

    out_ref[0, :, :ND] = made[:, :ND].astype(jnp.bfloat16)
    out_ref[0, :, ND:] = rotated(made[:, ND : ND + LANES]).astype(jnp.bfloat16)
    second = ND + RD
    out_ref[1, :, :ND] = made[:, second : second + ND].astype(jnp.bfloat16)
    rope = pltpu.roll(made[:, second + RD : second + RD + LANES], RD, 1)
    out_ref[1, :, ND:] = rotated(rope).astype(jnp.bfloat16)


def attend_kernel(n_pieces, first, last, *refs):
    q_ref, key_pos, query_pos, query_start, w_ref = refs[:5]
    pieces = refs[5 : 5 + n_pieces]
    at = 5 + n_pieces
    if not first:
        max_in, sum_in, acc_in = refs[at : at + 3]
        at += 3
    if last:
        (out_ref,) = refs[at : at + 1]
        at += 1
    else:
        max_out, sum_out, acc_out = refs[at : at + 3]
        at += 3
    rows_ref, rope_ref, bias_ref = refs[at:]
    size = pieces[0].shape[0]

    @pl.when(pl.program_id(0) == 0)
    def _():
        for n, ref in enumerate(pieces):
            low = pl.ds(n * size, size)
            high = pl.ds((n_pieces + n) * size, size)
            rows_ref[low, :] = ref[:, :KL]
            rows_ref[high, :] = ref[:, KL : 2 * KL]
            rope = ref[:, 2 * KL :]
            rope_ref[low, :] = rope
            rope_ref[high, :] = jnp.concatenate([rope[:, RD:], rope[:, :RD]], axis=1)
        allowed = (key_pos[...] <= query_pos[...]) & (key_pos[...] >= query_start[...])
        bias_ref[...] = jnp.where(allowed, 0.0, MASKED)

    for head in range(q_ref.shape[0]):
        w = w_ref[:, head * (ND + VD) : (head + 1) * (ND + VD)]
        expanded = jnp.dot(rows_ref[...], w, preferred_element_type=jnp.float32)
        expanded = expanded.astype(jnp.bfloat16)
        keys = jnp.concatenate([expanded[:, :ND], rope_ref[...]], axis=1)
        scores = lax.dot_general(
            q_ref[head], keys, (((1,), (1,)), ((), ())), preferred_element_type=jnp.float32
        )
        scores = scores * SCORE_SCALE + bias_ref[...]
        top = jnp.max(scores, axis=1, keepdims=True)
        if first:
            new_max = jnp.maximum(top, FLOOR)
        else:
            old_max = max_in[head][:, :1]
            new_max = jnp.maximum(top, old_max)
        weights = jnp.exp2(scores - new_max)
        total = jnp.sum(weights, axis=1, keepdims=True)
        mixed = jnp.dot(
            weights.astype(jnp.bfloat16), expanded[:, ND:], preferred_element_type=jnp.float32
        )
        if not first:
            faded = jnp.exp2(old_max - new_max)
            total = total + faded * sum_in[head][:, :1]
            mixed = mixed + faded * acc_in[head]
        if last:
            out_ref[:, head * VD : (head + 1) * VD] = (mixed / total).astype(jnp.bfloat16)
        else:
            max_out[head] = jnp.broadcast_to(new_max, mixed.shape)
            sum_out[head] = jnp.broadcast_to(total, mixed.shape)
            acc_out[head] = mixed


def attend(queries, key_pos, query_pos, query_start, w_kv, pieces, state, last):
    heads, rows, width = queries.shape
    group = 2
    first = state is None
    count = key_pos.shape[1]

    def whole(a):
        return pl.BlockSpec(a.shape, lambda h: (0,) * a.ndim)

    part = pl.BlockSpec((group, rows, VD), lambda h: (h, 0, 0))
    in_specs = [
        pl.BlockSpec((group, rows, width), lambda h: (h, 0, 0)),
        whole(key_pos),
        whole(query_pos),
        whole(query_start),
        pl.BlockSpec((KL, group * (ND + VD)), lambda h: (0, h)),
        *[whole(p) for p in pieces],
    ]
    args = [queries, key_pos, query_pos, query_start, w_kv, *pieces]
    if not first:
        in_specs += [part] * 3
        args += list(state)
    if last:
        out_shape = jax.ShapeDtypeStruct((rows, heads * VD), jnp.bfloat16)
        out_specs = pl.BlockSpec((rows, group * VD), lambda h: (0, h))
    else:
        out_shape = [jax.ShapeDtypeStruct((heads, rows, VD), jnp.float32)] * 3
        out_specs = [part] * 3

    def kernel(*refs):
        attend_kernel(len(pieces), first, last, *refs)

    return pl.pallas_call(
        kernel,
        grid=(heads // group,),
        in_specs=in_specs,
        out_specs=out_specs,
        out_shape=out_shape,
        scratch_shapes=[
            pltpu.VMEM((count, KL), jnp.bfloat16),
            pltpu.VMEM((count, LANES), jnp.bfloat16),
            pltpu.VMEM((rows, count), jnp.float32),
        ],
        compiler_params=pltpu.CompilerParams(vmem_limit_bytes=48 * 2**20),
    )(*args)


def body(q_latent, q_gain, kv_cache, kv_gain, w_query, w_kv, doc_lengths):
    ctx_size, head_size = lax.axis_size("ctx"), lax.axis_size("head")
    chips, ys = ctx_size // 2, head_size // 2
    reach = chips // 4
    mine = q_latent.shape[0]
    tok_dev = mine * head_size
    heads_here = w_query.shape[1] // (ND + RD)
    ctx, head = lax.axis_index("ctx"), lax.axis_index("head")
    chip, core, y, xh = ctx // 2, ctx % 2, head // 2, head % 2

    swap = [(n, n ^ 1) for n in range(ctx_size)]
    across_x = [(n, n ^ 1) for n in range(head_size)]

    def chip_shift(step):
        return [
            (2 * n + c, 2 * ((n + step + reach * c) % chips) + c)
            for n in range(chips)
            for c in range(2)
        ]

    def y_shift(step):
        return [(2 * n + x, 2 * ((n + step) % ys) + x) for n in range(ys) for x in range(2)]

    q_rows, kv_rows = pl.pallas_call(
        norm_kernel,
        out_shape=[
            jax.ShapeDtypeStruct(q_latent.shape, jnp.bfloat16),
            jax.ShapeDtypeStruct(kv_cache.shape, jnp.bfloat16),
        ],
    )(q_latent, q_gain[None, :], kv_cache, kv_gain[None, :])

    kv_other = lax.ppermute(kv_rows, "head", across_x)
    q_other = lax.ppermute(q_rows, "head", across_x)

    piece = jnp.concatenate(
        [kv_rows[:, :KL], kv_other[:, :KL], kv_rows[:, KL:], kv_other[:, KL:]], axis=1
    )
    swapped = lax.ppermute(piece, "ctx", swap)
    even = jnp.where(core == 0, piece, swapped)
    odd = jnp.where(core == 0, swapped, piece)
    pair = jnp.concatenate([even, odd], axis=0)
    window = [lax.ppermute(pair, "ctx", chip_shift(step)) for step in range(1, reach + 1)]

    q_pair = jnp.concatenate([q_rows, q_other], axis=0)
    q_after = lax.ppermute(q_pair, "head", y_shift(1))
    q_before = lax.ppermute(q_pair, "head", y_shift(-1))
    q_across = lax.ppermute(q_pair, "head", y_shift(2))

    held = jnp.concatenate([piece, *window], axis=0)
    from_after = lax.ppermute(held, "head", y_shift(1))
    from_before = lax.ppermute(held, "head", y_shift(-1))
    from_across = lax.ppermute(held, "head", y_shift(2))

    query_pos = ctx * tok_dev + jnp.arange(tok_dev, dtype=jnp.int32)
    doc_end = jnp.zeros((), jnp.int32)
    query_start = jnp.zeros_like(query_pos)
    for doc in range(doc_lengths.shape[0]):
        doc_end = doc_end + doc_lengths[doc]
        query_start = query_start + jnp.where(query_pos >= doc_end, doc_lengths[doc], 0)
    half_width = RD // 2
    freq_index = jnp.arange(half_width, dtype=jnp.float32)
    frequency = jnp.exp(freq_index * (-2.0 * math.log(10000.0) / RD))
    angles = (query_pos - query_start).astype(jnp.float32)[:, None] * frequency[None, :]
    cosine, sine = jnp.cos(angles), jnp.sin(angles)
    blank = jnp.zeros((tok_dev, LANES - RD), jnp.float32)
    cos_table = jnp.concatenate([cosine, cosine, blank], axis=1)
    sin_table = jnp.concatenate([-sine, sine, blank], axis=1)

    sources = [y, (y - 1) % ys, (y + 1) % ys, (y + 2) % ys]
    places = jnp.stack([s * 2 * mine + x * mine for s in sources for x in (xh, 1 - xh)])
    row_spec = pl.BlockSpec(q_pair.shape, lambda h, *_: (0, 0))
    table_spec = pl.BlockSpec(cos_table.shape, lambda h, *_: (0, 0))
    pair_width = 2 * (ND + RD)
    queries = pl.pallas_call(
        query_kernel,
        grid_spec=pltpu.PrefetchScalarGridSpec(
            num_scalar_prefetch=1,
            grid=(heads_here // 2,),
            in_specs=[row_spec] * 4
            + [table_spec] * 2
            + [pl.BlockSpec((w_query.shape[0], pair_width), lambda h, *_: (0, h))],
            out_specs=pl.BlockSpec((2, tok_dev, 2 * LANES), lambda h, *_: (h, 0, 0)),
            scratch_shapes=[pltpu.VMEM((tok_dev, w_query.shape[0]), jnp.bfloat16)],
        ),
        out_shape=jax.ShapeDtypeStruct((heads_here, tok_dev, 2 * LANES), jnp.bfloat16),
        compiler_params=pltpu.CompilerParams(vmem_limit_bytes=48 * 2**20),
    )(places, q_pair, q_after, q_before, q_across, cos_table, sin_table, w_query)

    def held_rows(c):
        rows = [c * tok_dev + np.arange(mine)]
        for step in range(1, reach + 1):
            for parity in range(2):
                rows.append((parity - 2 * (step + reach * c)) * tok_dev + np.arange(mine))
        return np.concatenate(rows).astype(np.int32)

    table = np.stack([held_rows(0), held_rows(1)])
    own_rows = jnp.where(core == 0, table[0], table[1]) + 2 * chip * tok_dev
    partner_rows = jnp.where(core == 0, table[1], table[0]) + 2 * chip * tok_dev

    def key_positions(which):
        halves = []
        for x in (xh, 1 - xh):
            for s in which:
                for rows in (own_rows, partner_rows):
                    halves.append(rows + s * 2 * mine + x * mine)
        return jnp.concatenate(halves)[None, :]

    at = (query_pos[:, None], query_start[:, None], w_kv)

    own_swapped = lax.ppermute(held, "ctx", swap)
    state = attend(queries, key_positions(sources[:1]), *at, [held, own_swapped], None, False)
    after_swapped = lax.ppermute(from_after, "ctx", swap)
    before_swapped = lax.ppermute(from_before, "ctx", swap)
    near = [from_after, after_swapped, from_before, before_swapped]
    state = attend(queries, key_positions(sources[1:3]), *at, near, state, False)
    across_swapped = lax.ppermute(from_across, "ctx", swap)
    far = [from_across, across_swapped]
    return attend(queries, key_positions(sources[3:]), *at, far, state, True)


def solution(mesh):
    placed = (
        P(("ctx", "head"), None),
        P(),
        P(("ctx", "head"), None),
        P(),
        P(None, "head"),
        P(None, "head"),
        P(),
    )
    return jax.shard_map(
        body, mesh=mesh, in_specs=placed, out_specs=P("ctx", "head"), check_vma=False
    )
```

```python
import math

import jax
import jax.numpy as jnp
import numpy as np
from jax import lax
from jax.experimental import pallas as pl
from jax.experimental.pallas import tpu as pltpu
from jax.sharding import PartitionSpec as P

KL = 512
RD = 64
ND = 128
VD = 128
LANES = 128
EPSILON = 1e-06
MASKED = -1e30
FLOOR = -1e29
COARSE = (1, 4, 7)
SCORE_SCALE = math.log2(math.e) / math.sqrt(ND + RD)


def scaled(values, gain):
    mean = jnp.mean(values * values, axis=-1, keepdims=True)
    return values * lax.rsqrt(mean + EPSILON) * gain


def norm_q_kernel(rows_ref, gain_ref, out_ref):
    rows = rows_ref[...].astype(jnp.float32)
    out_ref[...] = scaled(rows, gain_ref[...][None, :]).astype(jnp.bfloat16)


def norm_kv_kernel(rows_ref, gain_ref, out_ref):
    latent = rows_ref[:, :KL].astype(jnp.float32)
    out_ref[:, :KL] = scaled(latent, gain_ref[...][None, :]).astype(jnp.bfloat16)
    out_ref[:, KL:] = rows_ref[:, KL:]


def pair_kernel(spot, own_ref, other_ref, out_ref):
    def lay(even, odd):
        out_ref[:, :KL] = even[:, :KL]
        out_ref[:, KL : 2 * KL] = odd[:, :KL]
        out_ref[:, 2 * KL :] = jnp.concatenate([even[:, KL:], odd[:, KL:]], axis=1)

    @pl.when(spot[1] == 0)
    def _():
        lay(own_ref, other_ref)

    @pl.when(spot[1] != 0)
    def _():
        lay(other_ref, own_ref)


def join_kernel(sizes, n_after, *refs):
    outs = refs[len(refs) - len(sizes) :]
    at = 0
    for size, out_ref in zip(sizes, outs):
        row = 0
        for ref in refs[at : at + size]:
            out_ref[row : row + ref.shape[0], :] = ref[...]
            row += ref.shape[0]
        at += size


def join(groups, after=()):
    sizes = [len(g) for g in groups]
    shapes = [
        jax.ShapeDtypeStruct((sum(a.shape[0] for a in g), g[0].shape[1]), g[0].dtype)
        for g in groups
    ]
    arrays = [a for g in groups for a in g]
    vmem = pl.BlockSpec(memory_space=pltpu.VMEM)
    anywhere = pl.BlockSpec(memory_space=pl.ANY)

    def kernel(*refs):
        join_kernel(sizes, len(after), *refs)

    return pl.pallas_call(
        kernel,
        in_specs=[vmem] * len(arrays) + [anywhere] * len(after),
        out_specs=[vmem] * len(groups),
        out_shape=shapes,
    )(*arrays, *after)


def query_kernel(spot, own, after, before, across, cos_ref, sin_ref, w_ref, out_ref, rows_ref):
    y, xh = spot[2], spot[3]
    for shift, ref in ((0, own), (3, after), (1, before), (2, across)):
        for half in range(2):
            place = lax.rem(y + shift, 4) * 32 + lax.rem(xh + half, 2) * 16
            at = pl.multiple_of(place, 16)
            rows_ref[pl.ds(at, 16), :] = ref[16 * half : 16 * half + 16, :]

    lane = lax.broadcasted_iota(jnp.int32, (rows_ref.shape[0], LANES), 1)

    def rotated(rope):
        turned = jnp.where(
            lane < RD // 2, pltpu.roll(rope, LANES - RD // 2, 1), pltpu.roll(rope, RD // 2, 1)
        )
        return rope * cos_ref[...] + turned * sin_ref[...]

    width = 2 * (ND + RD)
    for pair in range(w_ref.shape[1] // width):
        w = w_ref[:, pair * width : (pair + 1) * width]
        made = jnp.dot(rows_ref[...], w, preferred_element_type=jnp.float32)
        out_ref[2 * pair, :, :ND] = made[:, :ND].astype(jnp.bfloat16)
        out_ref[2 * pair, :, ND:] = rotated(made[:, ND : ND + LANES]).astype(jnp.bfloat16)
        second = ND + RD
        out_ref[2 * pair + 1, :, :ND] = made[:, second : second + ND].astype(jnp.bfloat16)
        rope = pltpu.roll(made[:, second + RD : second + RD + LANES], RD, 1)
        out_ref[2 * pair + 1, :, ND:] = rotated(rope).astype(jnp.bfloat16)


def attend_kernel(n_pieces, shifts, first, last, *refs):
    spot, q_ref, table_ref, w_ref = refs[:4]
    pieces = refs[4 : 4 + n_pieces]
    at = 4 + n_pieces
    if not first:
        max_in, sum_in, acc_in = refs[at : at + 3]
        at += 3
    if last:
        (out_ref,) = refs[at : at + 1]
        at += 1
    else:
        max_out, sum_out, acc_out = refs[at : at + 3]
        at += 3
    rows_ref, rope_ref, bias_ref = refs[at:]
    size = pieces[0].shape[0]

    for n, ref in enumerate(pieces):
        low = pl.ds(n * size, size)
        high = pl.ds((n_pieces + n) * size, size)
        rows_ref[low, :] = ref[:, :KL]
        rows_ref[high, :] = ref[:, KL : 2 * KL]
        rope = ref[:, 2 * KL :]
        rope_ref[low, :] = rope
        rope_ref[high, :] = jnp.concatenate([rope[:, RD:], rope[:, :RD]], axis=1)

    chip, core, y, xh = spot[0], spot[1], spot[2], spot[3]
    tok_dev, n_keys = bias_ref.shape
    query_pos = (2 * chip + core) * tok_dev + lax.broadcasted_iota(jnp.int32, (tok_dev, 1), 0)
    query_start = jnp.zeros_like(query_pos)
    for doc in range(4, spot.shape[0]):
        query_start = jnp.where(query_pos >= spot[doc], spot[doc], query_start)
    ys = jnp.where(
        table_ref[2:3, :] == 0, lax.rem(y + shifts[0], 4), lax.rem(y + shifts[-1], 4)
    )
    xs = jnp.where(table_ref[1:2, :] == 0, lax.rem(xh + core, 2), lax.rem(xh + core + 1, 2))
    key_pos = table_ref[0:1, :] + 2 * chip * tok_dev + ys * 32 + xs * 16
    allowed = (key_pos <= query_pos) & (key_pos >= query_start)
    bias_ref[...] = jnp.where(allowed, 0.0, MASKED)

    for head in range(q_ref.shape[0]):
        w = w_ref[:, head * (ND + VD) : (head + 1) * (ND + VD)]
        expanded = jnp.dot(rows_ref[...], w, preferred_element_type=jnp.float32)
        expanded = expanded.astype(jnp.bfloat16)
        keys = jnp.concatenate([expanded[:, :ND], rope_ref[...]], axis=1)
        scores = lax.dot_general(
            q_ref[head], keys, (((1,), (1,)), ((), ())), preferred_element_type=jnp.float32
        )
        scores = scores * SCORE_SCALE + bias_ref[...]
        top = jnp.max(scores, axis=1, keepdims=True)
        if first:
            new_max = jnp.maximum(top, FLOOR)
        else:
            old_max = max_in[head][:, :1]
            new_max = jnp.maximum(top, old_max)
        weights = jnp.exp2(scores - new_max)
        total = jnp.sum(weights, axis=1, keepdims=True)
        mixed = jnp.dot(
            weights.astype(jnp.bfloat16), expanded[:, ND:], preferred_element_type=jnp.float32
        )
        if not first:
            faded = jnp.exp2(old_max - new_max)
            total = total + faded * sum_in[head][:, :1]
            mixed = mixed + faded * acc_in[head]
        if last:
            out_ref[:, head * VD : (head + 1) * VD] = (mixed / total).astype(jnp.bfloat16)
        else:
            max_out[head] = jnp.broadcast_to(new_max, mixed.shape)
            sum_out[head] = jnp.broadcast_to(total, mixed.shape)
            acc_out[head] = mixed


def key_table(slots, rows, tok_dev, n_sources):
    held = np.concatenate([np.arange(rows) - 2 * k * tok_dev for k in slots])
    columns = []
    for parity in range(2):
        for source in range(n_sources):
            for partner in range(2):
                place = held + parity * tok_dev
                columns.append(np.stack([place, 0 * place + partner, 0 * place + source]))
    return np.concatenate(columns, axis=1).astype(np.int32)


def attend(spot, queries, slots, w_kv, pieces, shifts, state, last):
    heads, rows, width = queries.shape
    first = state is None
    table = jnp.asarray(key_table(slots, 16, rows, len(shifts)))
    count = table.shape[1]
    vmem = pl.BlockSpec(memory_space=pltpu.VMEM)
    args = [spot, queries, table, w_kv, *pieces]
    if not first:
        args += list(state)
    if last:
        out_shape = jax.ShapeDtypeStruct((rows, heads * VD), jnp.bfloat16)
        out_specs = vmem
    else:
        out_shape = [jax.ShapeDtypeStruct((heads, rows, VD), jnp.float32)] * 3
        out_specs = [vmem] * 3

    def kernel(*refs):
        attend_kernel(len(pieces), shifts, first, last, *refs)

    return pl.pallas_call(
        kernel,
        in_specs=[pl.BlockSpec(memory_space=pltpu.SMEM)] + [vmem] * (len(args) - 1),
        out_specs=out_specs,
        out_shape=out_shape,
        scratch_shapes=[
            pltpu.VMEM((count, KL), jnp.bfloat16),
            pltpu.VMEM((count, LANES), jnp.bfloat16),
            pltpu.VMEM((rows, count), jnp.float32),
        ],
        compiler_params=pltpu.CompilerParams(vmem_limit_bytes=48 * 2**20),
    )(*args)


def body(q_latent, q_gain, kv_cache, kv_gain, w_query, w_kv, doc_lengths):
    ctx_size, head_size = lax.axis_size("ctx"), lax.axis_size("head")
    chips, ys = ctx_size // 2, head_size // 2
    tok_dev = q_latent.shape[0] * head_size
    heads_here = w_query.shape[1] // (ND + RD)
    ctx, head = lax.axis_index("ctx"), lax.axis_index("head")
    smem, vmem = pl.BlockSpec(memory_space=pltpu.SMEM), pl.BlockSpec(memory_space=pltpu.VMEM)

    swap = [(n, n ^ 1) for n in range(ctx_size)]
    across_x = [(n, n ^ 1) for n in range(head_size)]

    def chip_shift(step):
        return [(2 * n + c, 2 * ((n + step) % chips) + c) for n in range(chips) for c in range(2)]

    def coarse_shift(step):
        return [
            ((2 * n + c) * head_size + h, (2 * ((n + step) % chips) + c) * head_size + (h ^ c))
            for n in range(chips)
            for c in range(2)
            for h in range(head_size)
        ]

    def y_shift(step):
        return [(2 * n + x, 2 * ((n + step) % ys) + x) for n in range(ys) for x in range(2)]

    ends = [doc_lengths[0]]
    for doc in range(1, doc_lengths.shape[0]):
        ends.append(ends[-1] + doc_lengths[doc])
    spot = jnp.stack([ctx // 2, ctx % 2, head // 2, head % 2, *ends])

    kv_rows = pl.pallas_call(
        norm_kv_kernel, out_shape=jax.ShapeDtypeStruct(kv_cache.shape, jnp.bfloat16)
    )(kv_cache, kv_gain)
    kv_other = lax.ppermute(kv_rows, "ctx", swap)
    piece = pl.pallas_call(
        pair_kernel,
        in_specs=[smem, vmem, vmem],
        out_specs=vmem,
        out_shape=jax.ShapeDtypeStruct((kv_rows.shape[0], 2 * kv_rows.shape[1]), jnp.bfloat16),
    )(spot, kv_rows, kv_other)
    coarse = [lax.ppermute(piece, ("ctx", "head"), coarse_shift(step)) for step in COARSE]

    q_rows = pl.pallas_call(
        norm_q_kernel, out_shape=jax.ShapeDtypeStruct(q_latent.shape, jnp.bfloat16)
    )(q_latent, q_gain)
    q_other = lax.ppermute(q_rows, "head", across_x)

    coarse, q_pair = join([coarse, [q_rows, q_other]])
    later = lax.ppermute(coarse, "ctx", chip_shift(1))
    sooner = lax.ppermute(coarse, "ctx", chip_shift(-1))
    q_after = lax.ppermute(q_pair, "head", y_shift(1))
    q_before = lax.ppermute(q_pair, "head", y_shift(-1))
    q_across = lax.ppermute(q_pair, "head", y_shift(2))

    slots = [*COARSE, *[k + 1 for k in COARSE], *[k - 1 for k in COARSE]]
    (held,) = join([[coarse, later, sooner]], after=[q_after, q_before, q_across])
    from_after = lax.ppermute(held, "head", y_shift(1))
    from_before = lax.ppermute(held, "head", y_shift(-1))
    from_across = lax.ppermute(held, "head", y_shift(2))
    own_swapped = lax.ppermute(held, "ctx", swap)

    query_pos = ctx * tok_dev + jnp.arange(tok_dev, dtype=jnp.int32)
    query_start = jnp.zeros_like(query_pos)
    for end in ends:
        query_start = jnp.where(query_pos >= end, end, query_start)
    freq_index = jnp.arange(RD // 2, dtype=jnp.float32)
    frequency = jnp.exp(freq_index * (-2.0 * math.log(10000.0) / RD))
    angles = (query_pos - query_start).astype(jnp.float32)[:, None] * frequency[None, :]
    cosine, sine = jnp.cos(angles), jnp.sin(angles)
    blank = jnp.zeros((tok_dev, LANES - RD), jnp.float32)
    cos_table = jnp.concatenate([cosine, cosine, blank], axis=1)
    sin_table = jnp.concatenate([-sine, sine, blank], axis=1)

    queries = pl.pallas_call(
        query_kernel,
        in_specs=[smem] + [vmem] * 7,
        out_specs=vmem,
        out_shape=jax.ShapeDtypeStruct((heads_here, tok_dev, 2 * LANES), jnp.bfloat16),
        scratch_shapes=[pltpu.VMEM((tok_dev, w_query.shape[0]), jnp.bfloat16)],
        compiler_params=pltpu.CompilerParams(vmem_limit_bytes=48 * 2**20),
    )(spot, q_pair, q_after, q_before, q_across, cos_table, sin_table, w_query)

    state = attend(spot, queries, slots, w_kv, [held, own_swapped], [0], None, False)
    after_swapped = lax.ppermute(from_after, "ctx", swap)
    before_swapped = lax.ppermute(from_before, "ctx", swap)
    near = [from_after, after_swapped, from_before, before_swapped]
    state = attend(spot, queries, slots, w_kv, near, [3, 1], state, False)
    across_swapped = lax.ppermute(from_across, "ctx", swap)
    return attend(spot, queries, slots, w_kv, [from_across, across_swapped], [2], state, True)


def solution(mesh):
    placed = (
        P(("ctx", "head"), None),
        P(),
        P(("ctx", "head"), None),
        P(),
        P(None, "head"),
        P(None, "head"),
        P(),
    )
    return jax.shard_map(
        body, mesh=mesh, in_specs=placed, out_specs=P("ctx", "head"), check_vma=False
    )
```

```python
import math

import jax
import jax.numpy as jnp
import numpy as np
from jax import lax
from jax.experimental import pallas as pl
from jax.experimental.pallas import tpu as pltpu
from jax.sharding import PartitionSpec as P

KL = 512
RD = 64
ND = 128
VD = 128
LANES = 128
EPSILON = 1e-06
MASKED = -1e30
FLOOR = -1e29
COARSE = (1, 4, 7)
SCORE_SCALE = math.log2(math.e) / math.sqrt(ND + RD)


SMALL = pltpu.CompilerParams(vmem_limit_bytes=12 * 2**20)


def fast(array):
    return pltpu.with_memory_space_constraint(array, pltpu.VMEM)


def slow(array):
    return pltpu.with_memory_space_constraint(array, pltpu.HBM)


def here():
    ctx, head = lax.axis_index("ctx"), lax.axis_index("head")
    return ctx // 2, lax.rem(ctx, 2), head // 2, lax.rem(head, 2)


def scaled(values, gain):
    mean = jnp.mean(values * values, axis=-1, keepdims=True)
    return values * lax.rsqrt(mean + EPSILON) * gain


def norm_q_kernel(rows_ref, gain_ref, out_ref):
    rows = rows_ref[...].astype(jnp.float32)
    out_ref[...] = scaled(rows, gain_ref[...][None, :]).astype(jnp.bfloat16)


def norm_kv_kernel(rows_ref, gain_ref, out_ref):
    latent = rows_ref[:, :KL].astype(jnp.float32)
    out_ref[:, :KL] = scaled(latent, gain_ref[...][None, :]).astype(jnp.bfloat16)
    out_ref[:, KL:] = rows_ref[:, KL:]


def pair_kernel(own_ref, other_ref, out_ref):
    def lay(even, odd):
        out_ref[:, :KL] = even[:, :KL]
        out_ref[:, KL : 2 * KL] = odd[:, :KL]
        out_ref[:, 2 * KL :] = jnp.concatenate([even[:, KL:], odd[:, KL:]], axis=1)

    core = here()[1]

    @pl.when(core == 0)
    def _():
        lay(own_ref, other_ref)

    @pl.when(core != 0)
    def _():
        lay(other_ref, own_ref)


def join_kernel(sizes, n_after, *refs):
    outs = refs[len(refs) - len(sizes) :]
    at = 0
    for size, out_ref in zip(sizes, outs):
        row = 0
        for ref in refs[at : at + size]:
            out_ref[row : row + ref.shape[0], :] = ref[...]
            row += ref.shape[0]
        at += size


def join(groups, after=()):
    sizes = [len(g) for g in groups]
    shapes = [
        pltpu.VMEM((sum(a.shape[0] for a in g), g[0].shape[1]), g[0].dtype)
        for g in groups
    ]
    arrays = [a for g in groups for a in g]
    vmem = pl.BlockSpec(memory_space=pltpu.VMEM)

    def kernel(*refs):
        join_kernel(sizes, len(after), *refs)

    return pl.pallas_call(
        kernel,
        in_specs=[vmem] * (len(arrays) + len(after)),
        out_specs=[vmem] * len(groups),
        out_shape=shapes,
        compiler_params=SMALL,
    )(*[fast(a) for a in (*arrays, *after)])


def document_start(position, lengths):
    start, end = jnp.zeros_like(position), 0
    for doc in range(lengths.shape[0]):
        end = end + lengths[doc]
        start = jnp.where(position >= end, end, start)
    return start


def query_kernel(lengths, own, after, before, across, w_ref, out_ref, rows_ref):
    chip, core, y, xh = here()
    for shift, ref in ((0, own), (3, after), (1, before), (2, across)):
        for half in range(2):
            place = lax.rem(y + shift, 4) * 32 + lax.rem(xh + half, 2) * 16
            at = pl.multiple_of(place, 16)
            rows_ref[pl.ds(at, 16), :] = ref[16 * half : 16 * half + 16, :]

    shape = (rows_ref.shape[0], LANES)
    lane = lax.broadcasted_iota(jnp.int32, shape, 1)
    position = (2 * chip + core) * shape[0] + lax.broadcasted_iota(jnp.int32, shape, 0)
    offset = (position - document_start(position, lengths)).astype(jnp.float32)
    freq_index = lax.rem(lane, RD // 2).astype(jnp.float32)
    angles = offset * jnp.exp(freq_index * (-2.0 * math.log(10000.0) / RD))
    cosine = jnp.where(lane < RD, jnp.cos(angles), 0.0)
    sine = jnp.sin(angles)
    sine = jnp.where(lane < RD // 2, -sine, jnp.where(lane < RD, sine, 0.0))

    def rotated(rope):
        turned = jnp.where(
            lane < RD // 2, pltpu.roll(rope, LANES - RD // 2, 1), pltpu.roll(rope, RD // 2, 1)
        )
        return rope * cosine + turned * sine

    width = 2 * (ND + RD)
    for pair in range(w_ref.shape[1] // width):
        w = w_ref[:, pair * width : (pair + 1) * width]
        made = jnp.dot(rows_ref[...], w, preferred_element_type=jnp.float32)
        out_ref[2 * pair, :, :ND] = made[:, :ND].astype(jnp.bfloat16)
        out_ref[2 * pair, :, ND:] = rotated(made[:, ND : ND + LANES]).astype(jnp.bfloat16)
        second = ND + RD
        out_ref[2 * pair + 1, :, :ND] = made[:, second : second + ND].astype(jnp.bfloat16)
        rope = pltpu.roll(made[:, second + RD : second + RD + LANES], RD, 1)
        out_ref[2 * pair + 1, :, ND:] = rotated(rope).astype(jnp.bfloat16)


def attend_kernel(n_pieces, turn, first, last, *refs):
    lengths, q_ref, table_ref, w_ref = refs[:4]
    pieces = refs[4 : 4 + n_pieces]
    at = 4 + n_pieces
    if not first:
        max_in, sum_in, acc_in = refs[at : at + 3]
        at += 3
    if last:
        (out_ref,) = refs[at : at + 1]
        at += 1
    else:
        max_out, sum_out, acc_out = refs[at : at + 3]
        at += 3
    rows_ref, rope_ref, bias_ref = refs[at:]
    size = pieces[0].shape[0]

    for n, ref in enumerate(pieces):
        low = pl.ds(n * size, size)
        high = pl.ds((n_pieces + n) * size, size)
        rows_ref[low, :] = ref[:, :KL]
        rows_ref[high, :] = ref[:, KL : 2 * KL]
        rope = ref[:, 2 * KL :]
        rope_ref[low, :] = rope
        rope_ref[high, :] = jnp.concatenate([rope[:, RD:], rope[:, :RD]], axis=1)

    chip, core, y, xh = here()
    tok_dev, n_keys = bias_ref.shape
    query_pos = (2 * chip + core) * tok_dev + lax.broadcasted_iota(jnp.int32, (tok_dev, 1), 0)
    query_start = document_start(query_pos, lengths)
    ys = lax.rem(y + jnp.where(lax.rem(table_ref[1:2, :] + core, 2) == 0, 4 - turn, 4 + turn), 4)
    ys = lax.rem(ys + table_ref[2:3, :], 4)
    xs = lax.rem(xh + core + table_ref[1:2, :], 2)
    key_pos = table_ref[0:1, :] + 2 * chip * tok_dev + ys * 32 + xs * 16
    allowed = (key_pos <= query_pos) & (key_pos >= query_start)
    bias_ref[...] = jnp.where(allowed, 0.0, MASKED)

    for head in range(q_ref.shape[0]):
        w = w_ref[:, head * (ND + VD) : (head + 1) * (ND + VD)]
        expanded = jnp.dot(rows_ref[...], w, preferred_element_type=jnp.float32)
        expanded = expanded.astype(jnp.bfloat16)
        keys = jnp.concatenate([expanded[:, :ND], rope_ref[...]], axis=1)
        scores = lax.dot_general(
            q_ref[head], keys, (((1,), (1,)), ((), ())), preferred_element_type=jnp.float32
        )
        scores = scores * SCORE_SCALE + bias_ref[...]
        top = jnp.max(scores, axis=1, keepdims=True)
        if first:
            new_max = jnp.maximum(top, FLOOR)
        else:
            old_max = max_in[head][:, :1]
            new_max = jnp.maximum(top, old_max)
        weights = jnp.exp2(scores - new_max)
        total = jnp.sum(weights, axis=1, keepdims=True)
        mixed = jnp.dot(
            weights.astype(jnp.bfloat16), expanded[:, ND:], preferred_element_type=jnp.float32
        )
        if not first:
            faded = jnp.exp2(old_max - new_max)
            total = total + faded * sum_in[head][:, :1]
            mixed = mixed + faded * acc_in[head]
        if last:
            out_ref[:, head * VD : (head + 1) * VD] = (mixed / total).astype(jnp.bfloat16)
        else:
            max_out[head] = jnp.broadcast_to(new_max, mixed.shape)
            sum_out[head] = jnp.broadcast_to(total, mixed.shape)
            acc_out[head] = mixed


def key_table(slots, rows, tok_dev, partners):
    coarse = len(slots) // 3
    held = []
    for part in range(3):
        for turn in (0, 2):
            for k in slots[part * coarse : (part + 1) * coarse]:
                held += [(row - 2 * k * tok_dev, turn) for row in range(rows)]
    columns = [
        (place + parity * tok_dev, partner, turn)
        for parity in range(2)
        for partner in partners
        for place, turn in held
    ]
    return np.array(columns, np.int32).T


def attend(doc_lengths, queries, slots, w_kv, pieces, turn, partners, state, last):
    heads, rows, width = queries.shape
    first = state is None
    table = jnp.asarray(key_table(slots, 16, rows, partners))
    count = table.shape[1]
    vmem = pl.BlockSpec(memory_space=pltpu.VMEM)
    args = [queries, table, w_kv, *pieces]
    if not first:
        args += list(state)
    args = [slow(doc_lengths), *[fast(a) for a in args]]
    if last:
        out_shape = jax.ShapeDtypeStruct((rows, heads * VD), jnp.bfloat16)
        out_specs = vmem
    else:
        out_shape = [pltpu.VMEM((heads, rows, VD), jnp.float32)] * 3
        out_specs = [vmem] * 3

    def kernel(*refs):
        attend_kernel(len(pieces), turn, first, last, *refs)

    return pl.pallas_call(
        kernel,
        in_specs=[pl.BlockSpec(memory_space=pltpu.SMEM)] + [vmem] * (len(args) - 1),
        out_specs=out_specs,
        out_shape=out_shape,
        scratch_shapes=[
            pltpu.VMEM((count, KL), jnp.bfloat16),
            pltpu.VMEM((count, LANES), jnp.bfloat16),
            pltpu.VMEM((rows, count), jnp.float32),
        ],
        compiler_params=SMALL,
    )(*args)


def body(q_latent, q_gain, kv_cache, kv_gain, w_query, w_kv, doc_lengths):
    ctx_size, head_size = lax.axis_size("ctx"), lax.axis_size("head")
    chips, ys = ctx_size // 2, head_size // 2
    tok_dev = q_latent.shape[0] * head_size
    heads_here = w_query.shape[1] // (ND + RD)
    ctx, head = lax.axis_index("ctx"), lax.axis_index("head")
    vmem = pl.BlockSpec(memory_space=pltpu.VMEM)

    swap = [(n, n ^ 1) for n in range(ctx_size)]
    across_x = [(n, n ^ 1) for n in range(head_size)]

    def chip_shift(step):
        return [(2 * n + c, 2 * ((n + step) % chips) + c) for n in range(chips) for c in range(2)]

    def coarse_shift(step, turn):
        return [
            (
                (2 * n + c) * head_size + h,
                (2 * ((n + step) % chips) + c) * head_size + ((h + 2 * turn) % head_size ^ c),
            )
            for n in range(chips)
            for c in range(2)
            for h in range(head_size)
        ]

    apart = [
        ((2 * n + c) * head_size + h, (2 * n + c) * head_size + (h + 2 - 4 * c) % head_size)
        for n in range(chips)
        for c in range(2)
        for h in range(head_size)
    ]

    def y_shift(step):
        return [(2 * n + x, 2 * ((n + step) % ys) + x) for n in range(ys) for x in range(2)]

    kv_rows = pl.pallas_call(
        norm_kv_kernel,
        out_shape=pltpu.VMEM(kv_cache.shape, jnp.bfloat16),
        compiler_params=SMALL,

    )(slow(kv_cache), slow(kv_gain))
    q_rows = pl.pallas_call(
        norm_q_kernel,
        out_shape=pltpu.VMEM(q_latent.shape, jnp.bfloat16),
        compiler_params=SMALL,

    )(slow(q_latent), slow(q_gain))
    q_other = lax.ppermute(q_rows, "head", across_x)
    kv_other = lax.ppermute(kv_rows, "ctx", swap)
    piece = pl.pallas_call(
        pair_kernel,
        in_specs=[vmem, vmem],
        out_specs=vmem,
        out_shape=pltpu.VMEM((kv_rows.shape[0], 2 * kv_rows.shape[1]), jnp.bfloat16),
        compiler_params=SMALL,
    )(fast(kv_rows), fast(kv_other))
    coarse = [
        lax.ppermute(piece, ("ctx", "head"), coarse_shift(step, turn))
        for turn in (0, 2)
        for step in COARSE
    ]

    coarse, q_pair = join([coarse, [q_rows, q_other]])
    later = lax.ppermute(coarse, "ctx", chip_shift(1))
    sooner = lax.ppermute(coarse, "ctx", chip_shift(-1))
    q_after = lax.ppermute(q_pair, "head", y_shift(1))
    q_before = lax.ppermute(q_pair, "head", y_shift(-1))
    q_across = lax.ppermute(q_pair, "head", y_shift(2))

    slots = [*COARSE, *[k + 1 for k in COARSE], *[k - 1 for k in COARSE]]
    (held,) = join([[coarse, later, sooner]], after=[q_after, q_before, q_across])
    received = lax.ppermute(held, ("ctx", "head"), apart)
    own_swapped = lax.ppermute(held, "ctx", swap)

    queries = pl.pallas_call(
        query_kernel,
        in_specs=[pl.BlockSpec(memory_space=pltpu.SMEM)] + [vmem] * 5,
        out_specs=vmem,
        out_shape=pltpu.VMEM((heads_here, tok_dev, 2 * LANES), jnp.bfloat16),
        scratch_shapes=[pltpu.VMEM((tok_dev, w_query.shape[0]), jnp.bfloat16)],
        compiler_params=SMALL,
    )(slow(doc_lengths), *[fast(a) for a in (q_pair, q_after, q_before, q_across, w_query)])

    def attend_to(pieces, turn, partners, state, last=False):
        return attend(doc_lengths, queries, slots, w_kv, pieces, turn, partners, state, last)

    state = attend_to([held, own_swapped], 0, [0, 1], None)
    received, state = lax.optimization_barrier((received, state))
    swapped = lax.ppermute(received, "ctx", swap)
    state = attend_to([received], 1, [0], state)
    return attend_to([swapped], 1, [1], state, last=True)


def solution(mesh):
    placed = (
        P(("ctx", "head"), None),
        P(),
        P(("ctx", "head"), None),
        P(),
        P(None, "head"),
        P(None, "head"),
        P(),
    )
    return jax.shard_map(
        body, mesh=mesh, in_specs=placed, out_specs=P("ctx", "head"), check_vma=False
    )
```

```python
import math

import jax
import jax.numpy as jnp
import numpy as np
from jax import lax
from jax.experimental import pallas as pl
from jax.experimental.pallas import tpu as pltpu
from jax.sharding import PartitionSpec as P

KL = 512
RD = 64
ND = 128
VD = 128
LANES = 128
EPSILON = 1e-06
MASKED = -1e30
FLOOR = -1e29
COARSE = (1, 4, 7)
SCORE_SCALE = math.log2(math.e) / math.sqrt(ND + RD)


SMALL = pltpu.CompilerParams(vmem_limit_bytes=12 * 2**20)


def fast(array):
    return pltpu.with_memory_space_constraint(array, pltpu.VMEM)


def slow(array):
    return pltpu.with_memory_space_constraint(array, pltpu.HBM)


def here():
    ctx, head = lax.axis_index("ctx"), lax.axis_index("head")
    return ctx // 2, lax.rem(ctx, 2), head // 2, lax.rem(head, 2)


def scaled(values, gain):
    mean = jnp.mean(values * values, axis=-1, keepdims=True)
    return values * lax.rsqrt(mean + EPSILON) * gain


def norm_kernel(q_ref, q_gain_ref, kv_ref, kv_gain_ref, out_ref):
    latent = kv_ref[:, :KL].astype(jnp.float32)
    out_ref[:, :KL] = scaled(latent, kv_gain_ref[...][None, :]).astype(jnp.bfloat16)
    rows = q_ref[...].astype(jnp.float32)
    q_end = KL + rows.shape[1]
    out_ref[:, KL:q_end] = scaled(rows, q_gain_ref[...][None, :]).astype(jnp.bfloat16)
    out_ref[:, q_end:] = kv_ref[:, KL:]


def pair_kernel(own_ref, other_ref, out_ref):
    q_end = own_ref.shape[1] - RD
    q_size = q_end - KL
    at = 2 * (KL + RD)
    for n, ref in enumerate((own_ref, other_ref)):
        out_ref[:, n * KL : (n + 1) * KL] = ref[:, :KL]
        out_ref[:, at + n * q_size : at + (n + 1) * q_size] = ref[:, KL:q_end]
    rope = jnp.concatenate([own_ref[:, q_end:], other_ref[:, q_end:]], axis=1)
    out_ref[:, 2 * KL : at] = rope


def part_kernel(own_ref, got_ref, kv_ref, q_ref):
    size, width = own_ref.shape[0], kv_ref.shape[1]
    for n, ref in enumerate((own_ref, got_ref)):
        kv_ref[n * size : (n + 1) * size, :] = ref[:, :width]
        q_ref[n * size : (n + 1) * size, :] = ref[:, width:]


def join_kernel(sizes, n_after, *refs):
    outs = refs[len(refs) - len(sizes) :]
    at = 0
    for size, out_ref in zip(sizes, outs):
        row = 0
        for ref in refs[at : at + size]:
            out_ref[row : row + ref.shape[0], :] = ref[...]
            row += ref.shape[0]
        at += size


def join(groups, after=()):
    sizes = [len(g) for g in groups]
    shapes = [
        pltpu.VMEM((sum(a.shape[0] for a in g), g[0].shape[1]), g[0].dtype)
        for g in groups
    ]
    arrays = [a for g in groups for a in g]
    vmem = pl.BlockSpec(memory_space=pltpu.VMEM)

    def kernel(*refs):
        join_kernel(sizes, len(after), *refs)

    return pl.pallas_call(
        kernel,
        in_specs=[vmem] * (len(arrays) + len(after)),
        out_specs=[vmem] * len(groups),
        out_shape=shapes,
        compiler_params=SMALL,
    )(*[fast(a) for a in (*arrays, *after)])


def document_start(position, lengths):
    start, end = jnp.zeros_like(position), 0
    for doc in range(lengths.shape[0]):
        end = end + lengths[doc]
        start = jnp.where(position >= end, end, start)
    return start


def query_kernel(lengths, own, got, w_ref, out_ref, rows_ref):
    chip, core, y, xh = here()
    width = rows_ref.shape[1]
    for base, ref in ((y, own), (y + jnp.where(core == 0, 3, 1), got)):
        for n in range(4):
            turn, half = n // 2, n % 2
            place = lax.rem(base + 2 * turn, 4) * 32 + lax.rem(xh + half, 2) * 16
            at = pl.multiple_of(place, 16)
            rows = ref[16 * turn : 16 * turn + 16, half * width : (half + 1) * width]
            rows_ref[pl.ds(at, 16), :] = rows

    shape = (rows_ref.shape[0], LANES)
    lane = lax.broadcasted_iota(jnp.int32, shape, 1)
    position = (2 * chip + core) * shape[0] + lax.broadcasted_iota(jnp.int32, shape, 0)
    offset = (position - document_start(position, lengths)).astype(jnp.float32)
    freq_index = lax.rem(lane, RD // 2).astype(jnp.float32)
    angles = offset * jnp.exp(freq_index * (-2.0 * math.log(10000.0) / RD))
    cosine = jnp.where(lane < RD, jnp.cos(angles), 0.0)
    sine = jnp.sin(angles)
    sine = jnp.where(lane < RD // 2, -sine, jnp.where(lane < RD, sine, 0.0))

    def rotated(rope):
        turned = jnp.where(
            lane < RD // 2, pltpu.roll(rope, LANES - RD // 2, 1), pltpu.roll(rope, RD // 2, 1)
        )
        return rope * cosine + turned * sine

    width = 2 * (ND + RD)
    for pair in range(w_ref.shape[1] // width):
        w = w_ref[:, pair * width : (pair + 1) * width]
        made = jnp.dot(rows_ref[...], w, preferred_element_type=jnp.float32)
        out_ref[2 * pair, :, :ND] = made[:, :ND].astype(jnp.bfloat16)
        out_ref[2 * pair, :, ND:] = rotated(made[:, ND : ND + LANES]).astype(jnp.bfloat16)
        second = ND + RD
        out_ref[2 * pair + 1, :, :ND] = made[:, second : second + ND].astype(jnp.bfloat16)
        rope = pltpu.roll(made[:, second + RD : second + RD + LANES], RD, 1)
        out_ref[2 * pair + 1, :, ND:] = rotated(rope).astype(jnp.bfloat16)


def attend_kernel(n_pieces, turn, first, last, *refs):
    lengths, q_ref, table_ref, w_ref = refs[:4]
    pieces = refs[4 : 4 + n_pieces]
    at = 4 + n_pieces
    if not first:
        max_in, sum_in, acc_in = refs[at : at + 3]
        at += 3
    if last:
        (out_ref,) = refs[at : at + 1]
        at += 1
    else:
        max_out, sum_out, acc_out = refs[at : at + 3]
        at += 3
    rows_ref, rope_ref, bias_ref = refs[at:]
    size = pieces[0].shape[0]

    for n, ref in enumerate(pieces):
        low = pl.ds(n * size, size)
        high = pl.ds((n_pieces + n) * size, size)
        rows_ref[low, :] = ref[:, :KL]
        rows_ref[high, :] = ref[:, KL : 2 * KL]
        rope = ref[:, 2 * KL :]
        rope_ref[low, :] = rope
        rope_ref[high, :] = jnp.concatenate([rope[:, RD:], rope[:, :RD]], axis=1)

    chip, core, y, xh = here()
    tok_dev, n_keys = bias_ref.shape
    query_pos = (2 * chip + core) * tok_dev + lax.broadcasted_iota(jnp.int32, (tok_dev, 1), 0)
    query_start = document_start(query_pos, lengths)
    ys = lax.rem(y + jnp.where(lax.rem(table_ref[1:2, :] + core, 2) == 0, 4 - turn, 4 + turn), 4)
    ys = lax.rem(ys + table_ref[2:3, :], 4)
    xs = lax.rem(xh + table_ref[3:4, :], 2)
    parity = lax.rem(core + table_ref[1:2, :], 2)
    key_pos = table_ref[0:1, :] + (2 * chip + parity) * tok_dev + ys * 32 + xs * 16
    allowed = (key_pos <= query_pos) & (key_pos >= query_start)
    bias_ref[...] = jnp.where(allowed, 0.0, MASKED)

    for head in range(q_ref.shape[0]):
        w = w_ref[:, head * (ND + VD) : (head + 1) * (ND + VD)]
        expanded = jnp.dot(rows_ref[...], w, preferred_element_type=jnp.float32)
        expanded = expanded.astype(jnp.bfloat16)
        keys = jnp.concatenate([expanded[:, :ND], rope_ref[...]], axis=1)
        scores = lax.dot_general(
            q_ref[head], keys, (((1,), (1,)), ((), ())), preferred_element_type=jnp.float32
        )
        scores = scores * SCORE_SCALE + bias_ref[...]
        top = jnp.max(scores, axis=1, keepdims=True)
        if first:
            new_max = jnp.maximum(top, FLOOR)
        else:
            old_max = max_in[head][:, :1]
            new_max = jnp.maximum(top, old_max)
        weights = jnp.exp2(scores - new_max)
        total = jnp.sum(weights, axis=1, keepdims=True)
        mixed = jnp.dot(
            weights.astype(jnp.bfloat16), expanded[:, ND:], preferred_element_type=jnp.float32
        )
        if not first:
            faded = jnp.exp2(old_max - new_max)
            total = total + faded * sum_in[head][:, :1]
            mixed = mixed + faded * acc_in[head]
        if last:
            out_ref[:, head * VD : (head + 1) * VD] = (mixed / total).astype(jnp.bfloat16)
        else:
            max_out[head] = jnp.broadcast_to(new_max, mixed.shape)
            sum_out[head] = jnp.broadcast_to(total, mixed.shape)
            acc_out[head] = mixed


def key_table(slots, rows, tok_dev, partners):
    coarse = len(slots) // 3
    held = []
    for part in range(3):
        for k in slots[part * coarse : (part + 1) * coarse]:
            for turn in (0, 2):
                held += [(row - 2 * k * tok_dev, turn) for row in range(rows)]
    columns = [
        (place, partner, turn, half)
        for half in range(2)
        for partner in partners
        for place, turn in held
    ]
    return np.array(columns, np.int32).T


def attend(doc_lengths, queries, slots, w_kv, pieces, turn, partners, state, last):
    heads, rows, width = queries.shape
    first = state is None
    table = jnp.asarray(key_table(slots, 16, rows, partners))
    count = table.shape[1]
    vmem = pl.BlockSpec(memory_space=pltpu.VMEM)
    args = [queries, table, w_kv, *pieces]
    if not first:
        args += list(state)
    args = [slow(doc_lengths), *[fast(a) for a in args]]
    if last:
        out_shape = jax.ShapeDtypeStruct((rows, heads * VD), jnp.bfloat16)
        out_specs = vmem
    else:
        out_shape = [pltpu.VMEM((heads, rows, VD), jnp.float32)] * 3
        out_specs = [vmem] * 3

    def kernel(*refs):
        attend_kernel(len(pieces), turn, first, last, *refs)

    return pl.pallas_call(
        kernel,
        in_specs=[pl.BlockSpec(memory_space=pltpu.SMEM)] + [vmem] * (len(args) - 1),
        out_specs=out_specs,
        out_shape=out_shape,
        scratch_shapes=[
            pltpu.VMEM((count, KL), jnp.bfloat16),
            pltpu.VMEM((count, LANES), jnp.bfloat16),
            pltpu.VMEM((rows, count), jnp.float32),
        ],
        compiler_params=SMALL,
    )(*args)


def body(q_latent, q_gain, kv_cache, kv_gain, w_query, w_kv, doc_lengths):
    ctx_size, head_size = lax.axis_size("ctx"), lax.axis_size("head")
    chips, ys = ctx_size // 2, head_size // 2
    tok_dev = q_latent.shape[0] * head_size
    heads_here = w_query.shape[1] // (ND + RD)
    ctx, head = lax.axis_index("ctx"), lax.axis_index("head")
    vmem = pl.BlockSpec(memory_space=pltpu.VMEM)

    swap = [(n, n ^ 1) for n in range(ctx_size)]
    across_x = [(n, n ^ 1) for n in range(head_size)]

    def chip_shift(step):
        return [(2 * n + c, 2 * ((n + step) % chips) + c) for n in range(chips) for c in range(2)]

    apart = [
        ((2 * n + c) * head_size + h, (2 * n + c) * head_size + (h + 2 - 4 * c) % head_size)
        for n in range(chips)
        for c in range(2)
        for h in range(head_size)
    ]

    across_y = [(n, (n + ys) % head_size) for n in range(head_size)]

    size, q_width = q_latent.shape
    kv_width = kv_cache.shape[1]
    rows = pl.pallas_call(
        norm_kernel,
        out_shape=pltpu.VMEM((size, q_width + kv_width), jnp.bfloat16),
        compiler_params=SMALL,
    )(*[slow(a) for a in (q_latent, q_gain, kv_cache, kv_gain)])
    other = lax.ppermute(rows, "head", across_x)
    both = pl.pallas_call(
        pair_kernel,
        in_specs=[vmem] * 2,
        out_specs=vmem,
        out_shape=pltpu.VMEM((size, 2 * rows.shape[1]), jnp.bfloat16),
        compiler_params=SMALL,
    )(fast(rows), fast(other))
    opposite = lax.ppermute(both, "head", across_y)
    piece, q_set = pl.pallas_call(
        part_kernel,
        in_specs=[vmem] * 2,
        out_specs=[vmem] * 2,
        out_shape=[
            pltpu.VMEM((2 * size, 2 * kv_width), jnp.bfloat16),
            pltpu.VMEM((2 * size, 2 * q_width), jnp.bfloat16),
        ],
        compiler_params=SMALL,
    )(fast(both), fast(opposite))
    coarse = [lax.ppermute(piece, "ctx", chip_shift(step)) for step in COARSE]
    (coarse,) = join([coarse])
    later = lax.ppermute(coarse, "ctx", chip_shift(1))
    sooner = lax.ppermute(coarse, "ctx", chip_shift(-1))
    q_set, coarse = lax.optimization_barrier((q_set, coarse))
    q_got = lax.ppermute(q_set, ("ctx", "head"), apart)

    slots = [*COARSE, *[k + 1 for k in COARSE], *[k - 1 for k in COARSE]]
    (held,) = join([[coarse, later, sooner]], after=[q_got])
    received = lax.ppermute(held, ("ctx", "head"), apart)
    own_swapped = lax.ppermute(held, "ctx", swap)

    queries = pl.pallas_call(
        query_kernel,
        in_specs=[pl.BlockSpec(memory_space=pltpu.SMEM)] + [vmem] * 3,
        out_specs=vmem,
        out_shape=pltpu.VMEM((heads_here, tok_dev, 2 * LANES), jnp.bfloat16),
        scratch_shapes=[pltpu.VMEM((tok_dev, w_query.shape[0]), jnp.bfloat16)],
        compiler_params=SMALL,
    )(slow(doc_lengths), *[fast(a) for a in (q_set, q_got, w_query)])

    def attend_to(pieces, turn, partners, state, last=False):
        return attend(doc_lengths, queries, slots, w_kv, pieces, turn, partners, state, last)

    state = attend_to([held, own_swapped], 0, [0, 1], None)
    received, state = lax.optimization_barrier((received, state))
    swapped = lax.ppermute(received, "ctx", swap)
    state = attend_to([received], 1, [0], state)
    return attend_to([swapped], 1, [1], state, last=True)


def solution(mesh):
    placed = (
        P(("ctx", "head"), None),
        P(),
        P(("ctx", "head"), None),
        P(),
        P(None, "head"),
        P(None, "head"),
        P(),
    )
    return jax.shard_map(
        body, mesh=mesh, in_specs=placed, out_specs=P("ctx", "head"), check_vma=False
    )
```

```python
import math

import jax
import jax.numpy as jnp
import numpy as np
from jax import lax
from jax.experimental import pallas as pl
from jax.experimental.pallas import tpu as pltpu
from jax.sharding import PartitionSpec as P

KL = 512
RD = 64
ND = 128
VD = 128
LANES = 128
EPSILON = 1e-06
MASKED = -1e30
FLOOR = -1e29
COARSE = (1, 4, 7)
SCORE_SCALE = math.log2(math.e) / math.sqrt(ND + RD)


SMALL = pltpu.CompilerParams(vmem_limit_bytes=12 * 2**20)
LARGE = pltpu.CompilerParams(vmem_limit_bytes=28 * 2**20)


def fast(array):
    return pltpu.with_memory_space_constraint(array, pltpu.VMEM)


def slow(array):
    return pltpu.with_memory_space_constraint(array, pltpu.HBM)


def here():
    ctx, head = lax.axis_index("ctx"), lax.axis_index("head")
    return ctx // 2, lax.rem(ctx, 2), head // 2, lax.rem(head, 2)


def scaled(values, gain):
    mean = jnp.mean(values * values, axis=-1, keepdims=True)
    return values * lax.rsqrt(mean + EPSILON) * gain


def norm_kernel(q_ref, q_gain_ref, kv_ref, kv_gain_ref, out_ref):
    latent = kv_ref[:, :KL].astype(jnp.float32)
    out_ref[:, :KL] = scaled(latent, kv_gain_ref[...][None, :]).astype(jnp.bfloat16)
    rows = q_ref[...].astype(jnp.float32)
    q_end = KL + rows.shape[1]
    out_ref[:, KL:q_end] = scaled(rows, q_gain_ref[...][None, :]).astype(jnp.bfloat16)
    out_ref[:, q_end:] = kv_ref[:, KL:]


def pair_kernel(own_ref, other_ref, out_ref):
    q_end = own_ref.shape[1] - RD
    q_size = q_end - KL
    at = 2 * (KL + RD)
    for n, ref in enumerate((own_ref, other_ref)):
        out_ref[:, n * KL : (n + 1) * KL] = ref[:, :KL]
        out_ref[:, at + n * q_size : at + (n + 1) * q_size] = ref[:, KL:q_end]
    rope = jnp.concatenate([own_ref[:, q_end:], other_ref[:, q_end:]], axis=1)
    out_ref[:, 2 * KL : at] = rope


def part_kernel(own_ref, got_ref, kv_ref, q_ref):
    size, width = own_ref.shape[0], kv_ref.shape[1]
    for n, ref in enumerate((own_ref, got_ref)):
        kv_ref[n * size : (n + 1) * size, :] = ref[:, :width]
        q_ref[n * size : (n + 1) * size, :] = ref[:, width:]


def bundle_kernel(n_parts, *refs):
    *parts, q_ref, coarse_ref, bundle_ref = refs
    size, width = parts[0].shape
    for n, ref in enumerate(parts):
        coarse_ref[n * size : (n + 1) * size, :] = ref[...]
        bundle_ref[:, n * width : (n + 1) * width] = ref[...]
    bundle_ref[:, n_parts * width :] = q_ref[...]


def join_kernel(sizes, n_after, *refs):
    outs = refs[len(refs) - len(sizes) :]
    at = 0
    for size, out_ref in zip(sizes, outs):
        row = 0
        for ref in refs[at : at + size]:
            out_ref[row : row + ref.shape[0], :] = ref[...]
            row += ref.shape[0]
        at += size


def join(groups, after=()):
    sizes = [len(g) for g in groups]
    shapes = [
        pltpu.VMEM((sum(a.shape[0] for a in g), g[0].shape[1]), g[0].dtype)
        for g in groups
    ]
    arrays = [a for g in groups for a in g]
    vmem = pl.BlockSpec(memory_space=pltpu.VMEM)

    def kernel(*refs):
        join_kernel(sizes, len(after), *refs)

    return pl.pallas_call(
        kernel,
        in_specs=[vmem] * (len(arrays) + len(after)),
        out_specs=[vmem] * len(groups),
        out_shape=shapes,
        compiler_params=SMALL,
    )(*[fast(a) for a in (*arrays, *after)])


def document_start(position, lengths):
    start, end = jnp.zeros_like(position), 0
    for doc in range(lengths.shape[0]):
        end = end + lengths[doc]
        start = jnp.where(position >= end, end, start)
    return start


def query_kernel(q_at, lengths, own, got, w_hbm, out_ref, rows_ref, w_ref, arrived):
    fetches = []
    pairs, _, pair_width = w_ref.shape
    for n in range(pairs):
        columns = w_hbm.at[:, n * pair_width : (n + 1) * pair_width]
        fetches.append(pltpu.make_async_copy(columns, w_ref.at[n], arrived.at[n]))
        fetches[-1].start()
    chip, core, y, xh = here()
    width = rows_ref.shape[1]
    for base, ref, lane_at in ((y, own, 0), (y + jnp.where(core == 0, 3, 1), got, q_at)):
        for n in range(4):
            turn, half = n // 2, n % 2
            place = lax.rem(base + 2 * turn, 4) * 32 + lax.rem(xh + half, 2) * 16
            at = pl.multiple_of(place, 16)
            lanes = slice(lane_at + half * width, lane_at + (half + 1) * width)
            rows = ref[16 * turn : 16 * turn + 16, lanes]
            rows_ref[pl.ds(at, 16), :] = rows

    shape = (rows_ref.shape[0], LANES)
    lane = lax.broadcasted_iota(jnp.int32, shape, 1)
    position = (2 * chip + core) * shape[0] + lax.broadcasted_iota(jnp.int32, shape, 0)
    offset = (position - document_start(position, lengths)).astype(jnp.float32)
    freq_index = lax.rem(lane, RD // 2).astype(jnp.float32)
    angles = offset * jnp.exp(freq_index * (-2.0 * math.log(10000.0) / RD))
    cosine = jnp.where(lane < RD, jnp.cos(angles), 0.0)
    sine = jnp.sin(angles)
    sine = jnp.where(lane < RD // 2, -sine, jnp.where(lane < RD, sine, 0.0))

    def rotated(rope):
        turned = jnp.where(
            lane < RD // 2, pltpu.roll(rope, LANES - RD // 2, 1), pltpu.roll(rope, RD // 2, 1)
        )
        return rope * cosine + turned * sine

    for pair in range(pairs):
        fetches[pair].wait()
        made = jnp.dot(rows_ref[...], w_ref[pair], preferred_element_type=jnp.float32)
        out_ref[2 * pair, :, :ND] = made[:, :ND].astype(jnp.bfloat16)
        out_ref[2 * pair, :, ND:] = rotated(made[:, ND : ND + LANES]).astype(jnp.bfloat16)
        second = ND + RD
        out_ref[2 * pair + 1, :, :ND] = made[:, second : second + ND].astype(jnp.bfloat16)
        rope = pltpu.roll(made[:, second + RD : second + RD + LANES], RD, 1)
        out_ref[2 * pair + 1, :, ND:] = rotated(rope).astype(jnp.bfloat16)


def attend_kernel(views, group, first, last, *refs):
    lengths, q_ref, table_ref, w_ref = refs[:4]
    at = 4 + 1 + max(view[0] for view in views)
    pieces = refs[4:at]
    if not first:
        max_in, sum_in, acc_in = refs[at : at + 3]
        at += 3
    if last:
        (out_ref,) = refs[at : at + 1]
        at += 1
    else:
        max_out, sum_out, acc_out = refs[at : at + 3]
        at += 3
    rows_ref, rope_ref, bias_ref, made_ref, score_ref, weight_ref = refs[at:]
    heads = q_ref.shape[0]
    tok_dev, n_keys = bias_ref.shape

    row = 0
    for piece, lane_at, *_ in views:
        ref = pieces[piece]
        size = ref.shape[0]
        rope = ref[:, lane_at + 2 * KL : lane_at + 2 * (KL + RD)]
        turned = jnp.concatenate([rope[:, RD:], rope[:, :RD]], axis=1)
        for half in range(2):
            to = slice(row + half * (n_keys // 2), row + half * (n_keys // 2) + size)
            rows_ref[to, :] = ref[:, lane_at + half * KL : lane_at + (half + 1) * KL]
            rope_ref[to, :] = turned if half else rope
        row += size

    chip, core, y, xh = here()
    query_pos = (2 * chip + core) * tok_dev + lax.broadcasted_iota(jnp.int32, (tok_dev, 1), 0)
    query_start = document_start(query_pos, lengths)
    place, partner, turn, half, across = [table_ref[n : n + 1, :] for n in range(5)]
    holder = lax.rem(core + partner, 2)
    ys = lax.rem(y + turn + across * (3 - 2 * holder), 4)
    xs = lax.rem(xh + half, 2)
    key_pos = place + (2 * chip + holder) * tok_dev + ys * 32 + xs * 16
    allowed = (key_pos <= query_pos) & (key_pos >= query_start)
    bias_ref[...] = jnp.where(allowed, 0.0, MASKED)

    def expand(head):
        columns = slice(head * (ND + VD), (head + 1) * (ND + VD))
        made = jnp.dot(rows_ref[...], w_ref[:, columns], preferred_element_type=jnp.float32)
        made_ref[:, columns] = made.astype(jnp.bfloat16)

    def score(head):
        at = head * (ND + VD)
        keys = jnp.concatenate([made_ref[:, at : at + ND], rope_ref[...]], axis=1)
        scores = lax.dot_general(
            q_ref[head], keys, (((1,), (1,)), ((), ())), preferred_element_type=jnp.float32
        )
        score_ref[head] = scores * SCORE_SCALE + bias_ref[...]

    def weigh(head):
        scores = score_ref[head]
        top = jnp.max(scores, axis=1, keepdims=True)
        old_max = FLOOR if first else max_in[head][:, :1]
        new_max = jnp.maximum(top, old_max)
        weights = jnp.exp2(scores - new_max)
        total = jnp.sum(weights, axis=1, keepdims=True)
        weight_ref[head] = weights.astype(jnp.bfloat16)
        if first:
            return new_max, total, None
        faded = jnp.exp2(old_max - new_max)
        return new_max, total + faded * sum_in[head][:, :1], faded

    def mix(head, new_max, total, faded):
        at = head * (ND + VD) + ND
        values = made_ref[:, at : at + VD]
        mixed = jnp.dot(weight_ref[head], values, preferred_element_type=jnp.float32)
        if not first:
            mixed = mixed + faded * acc_in[head]
        if last:
            out_ref[:, head * VD : (head + 1) * VD] = (mixed * (1.0 / total)).astype(jnp.bfloat16)
        else:
            max_out[head] = jnp.broadcast_to(new_max, mixed.shape)
            sum_out[head] = jnp.broadcast_to(total, mixed.shape)
            acc_out[head] = mixed

    groups = [range(low, low + group) for low in range(0, heads, group)]
    found = {}
    for step in range(len(groups) + 3):
        if step < len(groups):
            for head in groups[step]:
                expand(head)
        if 0 <= step - 1 < len(groups):
            for head in groups[step - 1]:
                score(head)
        if 0 <= step - 2 < len(groups):
            for head in groups[step - 2]:
                found[head] = weigh(head)
        if 0 <= step - 3:
            for head in groups[step - 3]:
                mix(head, *found[head])


def key_table(views, rows, tok_dev):
    columns = []
    for half in range(2):
        for _, _, partner, across, slots in views:
            for k in slots:
                for turn in (0, 2):
                    place = [row - 2 * k * tok_dev for row in range(rows)]
                    columns += [(p, partner, turn, half, across) for p in place]
    return np.array(columns, np.int32).T


def attend(doc_lengths, queries, w_kv, pieces, views, group, state, last):
    heads, rows, width = queries.shape
    first = state is None
    table = jnp.asarray(key_table(views, 16, rows))
    count = table.shape[1]
    vmem = pl.BlockSpec(memory_space=pltpu.VMEM)
    args = [queries, table, w_kv, *pieces]
    if not first:
        args += list(state)
    args = [slow(doc_lengths), *[fast(a) for a in args]]
    if last:
        out_shape = jax.ShapeDtypeStruct((rows, heads * VD), jnp.bfloat16)
        out_specs = vmem
    else:
        out_shape = [pltpu.VMEM((heads, rows, VD), jnp.float32)] * 3
        out_specs = [vmem] * 3

    def kernel(*refs):
        attend_kernel(views, group, first, last, *refs)

    return pl.pallas_call(
        kernel,
        in_specs=[pl.BlockSpec(memory_space=pltpu.SMEM)] + [vmem] * (len(args) - 1),
        out_specs=out_specs,
        out_shape=out_shape,
        scratch_shapes=[
            pltpu.VMEM((count, KL), jnp.bfloat16),
            pltpu.VMEM((count, LANES), jnp.bfloat16),
            pltpu.VMEM((rows, count), jnp.float32),
            pltpu.VMEM((count, w_kv.shape[1]), jnp.bfloat16),
            pltpu.VMEM((heads, rows, count), jnp.float32),
            pltpu.VMEM((heads, rows, count), jnp.bfloat16),
        ],
        compiler_params=LARGE,
    )(*args)


def body(q_latent, q_gain, kv_cache, kv_gain, w_query, w_kv, doc_lengths):
    ctx_size, head_size = lax.axis_size("ctx"), lax.axis_size("head")
    chips, ys = ctx_size // 2, head_size // 2
    tok_dev = q_latent.shape[0] * head_size
    heads_here = w_query.shape[1] // (ND + RD)
    ctx, head = lax.axis_index("ctx"), lax.axis_index("head")
    vmem = pl.BlockSpec(memory_space=pltpu.VMEM)

    swap = [(n, n ^ 1) for n in range(ctx_size)]
    across_x = [(n, n ^ 1) for n in range(head_size)]

    def chip_shift(step):
        return [(2 * n + c, 2 * ((n + step) % chips) + c) for n in range(chips) for c in range(2)]

    apart = [
        ((2 * n + c) * head_size + h, (2 * n + c) * head_size + (h + 2 - 4 * c) % head_size)
        for n in range(chips)
        for c in range(2)
        for h in range(head_size)
    ]

    across_y = [(n, (n + ys) % head_size) for n in range(head_size)]

    size, q_width = q_latent.shape
    kv_width = kv_cache.shape[1]
    rows = pl.pallas_call(
        norm_kernel,
        out_shape=pltpu.VMEM((size, q_width + kv_width), jnp.bfloat16),
        compiler_params=SMALL,
    )(*[slow(a) for a in (q_latent, q_gain, kv_cache, kv_gain)])
    other = lax.ppermute(rows, "head", across_x)
    both = pl.pallas_call(
        pair_kernel,
        in_specs=[vmem] * 2,
        out_specs=vmem,
        out_shape=pltpu.VMEM((size, 2 * rows.shape[1]), jnp.bfloat16),
        compiler_params=SMALL,
    )(fast(rows), fast(other))
    opposite = lax.ppermute(both, "head", across_y)
    piece, q_set = pl.pallas_call(
        part_kernel,
        in_specs=[vmem] * 2,
        out_specs=[vmem] * 2,
        out_shape=[
            pltpu.VMEM((2 * size, 2 * kv_width), jnp.bfloat16),
            pltpu.VMEM((2 * size, 2 * q_width), jnp.bfloat16),
        ],
        compiler_params=SMALL,
    )(fast(both), fast(opposite))
    coarse = [lax.ppermute(piece, "ctx", chip_shift(step)) for step in COARSE]
    set_shape = coarse[0].shape
    q_at = len(COARSE) * set_shape[1]
    coarse, bundle = pl.pallas_call(
        lambda *refs: bundle_kernel(len(COARSE), *refs),
        in_specs=[vmem] * (len(COARSE) + 1),
        out_specs=[vmem] * 2,
        out_shape=[
            pltpu.VMEM((len(COARSE) * set_shape[0], set_shape[1]), jnp.bfloat16),
            pltpu.VMEM((set_shape[0], q_at + q_set.shape[1]), jnp.bfloat16),
        ],
        compiler_params=SMALL,
    )(*[fast(a) for a in (*coarse, q_set)])
    later = lax.ppermute(coarse, "ctx", chip_shift(1))
    sooner = lax.ppermute(coarse, "ctx", chip_shift(-1))
    got = lax.ppermute(bundle, ("ctx", "head"), apart)
    coarse_swapped = lax.ppermute(coarse, "ctx", swap)

    (near,) = join([[later, sooner]])
    received = lax.ppermute(near, ("ctx", "head"), apart)
    near_swapped = lax.ppermute(near, "ctx", swap)
    got_swapped = lax.ppermute(got, "ctx", swap)

    pairs = heads_here // 2
    queries = pl.pallas_call(
        lambda *refs: query_kernel(q_at, *refs),
        in_specs=[
            pl.BlockSpec(memory_space=pltpu.SMEM),
            vmem,
            vmem,
            pl.BlockSpec(memory_space=pl.ANY),
        ],
        out_specs=vmem,
        out_shape=pltpu.VMEM((heads_here, tok_dev, 2 * LANES), jnp.bfloat16),
        scratch_shapes=[
            pltpu.VMEM((tok_dev, w_query.shape[0]), jnp.bfloat16),
            pltpu.VMEM((pairs, w_query.shape[0], w_query.shape[1] // pairs), jnp.bfloat16),
            pltpu.SemaphoreType.DMA((pairs,)),
        ],
        compiler_params=SMALL,
    )(slow(doc_lengths), fast(q_set), fast(got), slow(w_query))

    def attend_to(pieces, views, group, state, last=False):
        return attend(doc_lengths, queries, w_kv, pieces, views, group, state, last)

    near_slots = [*[k + 1 for k in COARSE], *[k - 1 for k in COARSE]]
    views = [(0, 0, 0, 0, COARSE), (1, 0, 0, 0, near_slots)]
    views += [(2, 0, 1, 0, COARSE), (3, 0, 1, 0, near_slots)]
    for partner in range(2):
        for n, k in enumerate(COARSE):
            views.append((4 + partner, n * set_shape[1], partner, 1, [k]))
    pieces = [coarse, near, coarse_swapped, near_swapped, got, got_swapped]
    state = attend_to(pieces, views, 2, None)
    received, state = lax.optimization_barrier((received, state))
    swapped = lax.ppermute(received, "ctx", swap)
    state = attend_to([received], [(0, 0, 0, 1, near_slots)], 1, state)
    return attend_to([swapped], [(0, 0, 1, 1, near_slots)], 1, state, last=True)


def solution(mesh):
    placed = (
        P(("ctx", "head"), None),
        P(),
        P(("ctx", "head"), None),
        P(),
        P(None, "head"),
        P(None, "head"),
        P(),
    )
    return jax.shard_map(
        body, mesh=mesh, in_specs=placed, out_specs=P("ctx", "head"), check_vma=False
    )
```

```python
import math

import jax
import jax.numpy as jnp
import numpy as np
from jax import lax
from jax.experimental import pallas as pl
from jax.experimental.pallas import tpu as pltpu
from jax.sharding import PartitionSpec as P

KL = 512
RD = 64
ND = 128
VD = 128
LANES = 128
EPSILON = 1e-06
MASKED = -1e30
FLOOR = -1e29
COARSE = (4, 1, 7)
SCORE_SCALE = math.log2(math.e) / math.sqrt(ND + RD)


SMALL = pltpu.CompilerParams(vmem_limit_bytes=12 * 2**20)
LARGE = pltpu.CompilerParams(vmem_limit_bytes=28 * 2**20)


def fast(array):
    return pltpu.with_memory_space_constraint(array, pltpu.VMEM)


def slow(array):
    return pltpu.with_memory_space_constraint(array, pltpu.HBM)


def here():
    ctx, head = lax.axis_index("ctx"), lax.axis_index("head")
    return ctx // 2, lax.rem(ctx, 2), head // 2, lax.rem(head, 2)


def scaled(values, gain):
    mean = jnp.mean(values * values, axis=-1, keepdims=True)
    return values * lax.rsqrt(mean + EPSILON) * gain


def norm_kernel(q_ref, q_gain_ref, kv_ref, kv_gain_ref, out_ref):
    latent = kv_ref[:, :KL].astype(jnp.float32)
    out_ref[:, :KL] = scaled(latent, kv_gain_ref[...][None, :]).astype(jnp.bfloat16)
    rows = q_ref[...].astype(jnp.float32)
    q_end = KL + rows.shape[1]
    out_ref[:, KL:q_end] = scaled(rows, q_gain_ref[...][None, :]).astype(jnp.bfloat16)
    out_ref[:, q_end:] = kv_ref[:, KL:]


def split_kernel(w_ref, key_ref, value_ref):
    for head in range(key_ref.shape[0] // ND):
        at = head * (ND + VD)
        key_ref[head * ND : (head + 1) * ND, :] = w_ref[:, at : at + ND].T
        value_ref[:, head * VD : (head + 1) * VD] = w_ref[:, at + ND : at + ND + VD]


def fetch_kernel(from_ref, to_ref, arrived):
    pltpu.async_copy(from_ref, to_ref, arrived).wait()


def pair_kernel(own_ref, other_ref, ready_ref, out_ref):
    q_end = own_ref.shape[1] - RD
    q_size = q_end - KL
    at = 2 * (KL + RD)
    for n, ref in enumerate((own_ref, other_ref)):
        out_ref[:, n * KL : (n + 1) * KL] = ref[:, :KL]
        out_ref[:, at + n * q_size : at + (n + 1) * q_size] = ref[:, KL:q_end]
    rope = jnp.concatenate([own_ref[:, q_end:], other_ref[:, q_end:]], axis=1)
    out_ref[:, 2 * KL : at] = rope


def part_kernel(own_ref, got_ref, ready_ref, kv_ref, q_ref):
    size, width = own_ref.shape[0], kv_ref.shape[1]
    for n, ref in enumerate((own_ref, got_ref)):
        kv_ref[n * size : (n + 1) * size, :] = ref[:, :width]
        q_ref[n * size : (n + 1) * size, :] = ref[:, width:]


def bundle_kernel(n_parts, *refs):
    *parts, q_ref, coarse_ref, bundle_ref = refs
    size, width = parts[0].shape
    for n, ref in enumerate(parts):
        coarse_ref[n * size : (n + 1) * size, :] = ref[...]
        bundle_ref[:, n * width : (n + 1) * width] = ref[...]
    bundle_ref[:, n_parts * width :] = q_ref[...]


def join_kernel(sizes, n_after, *refs):
    outs = refs[len(refs) - len(sizes) :]
    at = 0
    for size, out_ref in zip(sizes, outs):
        row = 0
        for ref in refs[at : at + size]:
            out_ref[row : row + ref.shape[0], :] = ref[...]
            row += ref.shape[0]
        at += size


def join(groups, after=()):
    sizes = [len(g) for g in groups]
    shapes = [
        pltpu.VMEM((sum(a.shape[0] for a in g), g[0].shape[1]), g[0].dtype)
        for g in groups
    ]
    arrays = [a for g in groups for a in g]
    vmem = pl.BlockSpec(memory_space=pltpu.VMEM)

    def kernel(*refs):
        join_kernel(sizes, len(after), *refs)

    return pl.pallas_call(
        kernel,
        in_specs=[vmem] * (len(arrays) + len(after)),
        out_specs=[vmem] * len(groups),
        out_shape=shapes,
        compiler_params=SMALL,
    )(*[fast(a) for a in (*arrays, *after)])


def document_start(position, lengths):
    start, end = jnp.zeros_like(position), 0
    for doc in range(lengths.shape[0]):
        end = end + lengths[doc]
        start = jnp.where(position >= end, end, start)
    return start


def query_kernel(q_at, lengths, own, got, w_ref, out_ref, rows_ref):
    chip, core, y, xh = here()
    width = rows_ref.shape[1]
    for base, ref, lane_at in ((y, own, 0), (y + jnp.where(core == 0, 3, 1), got, q_at)):
        for n in range(4):
            turn, half = n // 2, n % 2
            place = lax.rem(base + 2 * turn, 4) * 32 + lax.rem(xh + half, 2) * 16
            at = pl.multiple_of(place, 16)
            lanes = slice(lane_at + half * width, lane_at + (half + 1) * width)
            rows = ref[16 * turn : 16 * turn + 16, lanes]
            rows_ref[pl.ds(at, 16), :] = rows

    shape = (rows_ref.shape[0], LANES)
    lane = lax.broadcasted_iota(jnp.int32, shape, 1)
    position = (2 * chip + core) * shape[0] + lax.broadcasted_iota(jnp.int32, shape, 0)
    offset = (position - document_start(position, lengths)).astype(jnp.float32)
    freq_index = lax.rem(lane, RD // 2).astype(jnp.float32)
    angles = offset * jnp.exp(freq_index * (-2.0 * math.log(10000.0) / RD))
    cosine = jnp.where(lane < RD, jnp.cos(angles), 0.0)
    sine = jnp.sin(angles)
    sine = jnp.where(lane < RD // 2, -sine, jnp.where(lane < RD, sine, 0.0))

    def rotated(rope):
        turned = jnp.where(
            lane < RD // 2, pltpu.roll(rope, LANES - RD // 2, 1), pltpu.roll(rope, RD // 2, 1)
        )
        return rope * cosine + turned * sine

    pair_width = 2 * (ND + RD)
    for pair in range(w_ref.shape[1] // pair_width):
        w = w_ref[:, pair * pair_width : (pair + 1) * pair_width]
        made = jnp.dot(rows_ref[...], w, preferred_element_type=jnp.float32)
        out_ref[2 * pair, :, :ND] = made[:, :ND].astype(jnp.bfloat16)
        out_ref[2 * pair, :, ND:] = rotated(made[:, ND : ND + LANES]).astype(jnp.bfloat16)
        second = ND + RD
        out_ref[2 * pair + 1, :, :ND] = made[:, second : second + ND].astype(jnp.bfloat16)
        rope = pltpu.roll(made[:, second + RD : second + RD + LANES], RD, 1)
        out_ref[2 * pair + 1, :, ND:] = rotated(rope).astype(jnp.bfloat16)


def attend_kernel(views, group, first, last, *refs):
    lengths, q_ref, table_ref, w_key_ref, w_value_ref = refs[:5]
    at = 5 + 1 + max(view[0] for view in views)
    pieces = refs[5:at]
    if not first:
        max_in, sum_in, acc_in = refs[at : at + 3]
        at += 3
    if last:
        (out_ref,) = refs[at : at + 1]
        at += 1
    else:
        max_out, sum_out, acc_out = refs[at : at + 3]
        at += 3
    rows_ref, rope_ref, bias_ref, turned_ref, key_ref, value_ref, score_ref, weight_ref = refs[at:]
    heads = q_ref.shape[0]
    tok_dev, n_keys = bias_ref.shape

    row = 0
    for piece, lane_at, *_ in views:
        ref = pieces[piece]
        size = ref.shape[0]
        rope = ref[:, lane_at + 2 * KL : lane_at + 2 * (KL + RD)]
        turned = jnp.concatenate([rope[:, RD:], rope[:, :RD]], axis=1)
        for half in range(2):
            to = slice(row + half * (n_keys // 2), row + half * (n_keys // 2) + size)
            rows_ref[to, :] = ref[:, lane_at + half * KL : lane_at + (half + 1) * KL]
            rope_ref[to, :] = turned if half else rope
        row += size

    chip, core, y, xh = here()
    query_pos = (2 * chip + core) * tok_dev + lax.broadcasted_iota(jnp.int32, (tok_dev, 1), 0)
    query_start = document_start(query_pos, lengths)
    place, partner, turn, half, across = [table_ref[n : n + 1, :] for n in range(5)]
    holder = lax.rem(core + partner, 2)
    ys = lax.rem(y + turn + across * (3 - 2 * holder), 4)
    xs = lax.rem(xh + half, 2)
    key_pos = place + (2 * chip + holder) * tok_dev + ys * 32 + xs * 16
    allowed = (key_pos <= query_pos) & (key_pos >= query_start)
    bias_ref[...] = jnp.where(allowed, 0.0, MASKED)

    turned_ref[:KL, :] = rows_ref[...].T
    turned_ref[KL:, :] = rope_ref[...].T

    def expand(pair):
        some = slice(pair * 2 * ND, (pair + 1) * 2 * ND)
        keys = jnp.dot(w_key_ref[some, :], turned_ref[:KL, :], preferred_element_type=jnp.float32)
        key_ref[some, :] = keys.astype(jnp.bfloat16)
        values = jnp.dot(rows_ref[...], w_value_ref[:, some], preferred_element_type=jnp.float32)
        value_ref[:, some] = values.astype(jnp.bfloat16)

    def score(head):
        keys = [key_ref[head * ND : (head + 1) * ND, :], turned_ref[KL:, :]]
        keys = jnp.concatenate(keys, axis=0)
        scores = jnp.dot(q_ref[head], keys, preferred_element_type=jnp.float32)
        score_ref[head] = scores * SCORE_SCALE + bias_ref[...]

    def weigh(head):
        scores = score_ref[head]
        top = jnp.max(scores, axis=1, keepdims=True)
        old_max = FLOOR if first else max_in[head][:, :1]
        new_max = jnp.maximum(top, old_max)
        weights = jnp.exp2(scores - new_max)
        total = jnp.sum(weights, axis=1, keepdims=True)
        weight_ref[head] = weights.astype(jnp.bfloat16)
        if first:
            return new_max, total, None
        faded = jnp.exp2(old_max - new_max)
        return new_max, total + faded * sum_in[head][:, :1], faded

    def mix(head, new_max, total, faded):
        values = value_ref[:, head * VD : (head + 1) * VD]
        mixed = jnp.dot(weight_ref[head], values, preferred_element_type=jnp.float32)
        if not first:
            mixed = mixed + faded * acc_in[head]
        if last:
            out_ref[:, head * VD : (head + 1) * VD] = (mixed * (1.0 / total)).astype(jnp.bfloat16)
        else:
            max_out[head] = jnp.broadcast_to(new_max, mixed.shape)
            sum_out[head] = jnp.broadcast_to(total, mixed.shape)
            acc_out[head] = mixed

    groups = [range(low, low + group) for low in range(0, heads, group)]
    found = {}
    for step in range(len(groups) + 3):
        if step < len(groups):
            for head in groups[step]:
                if head % 2 == 0:
                    expand(head // 2)
        if 0 <= step - 1 < len(groups):
            for head in groups[step - 1]:
                score(head)
        if 0 <= step - 2 < len(groups):
            for head in groups[step - 2]:
                found[head] = weigh(head)
        if 0 <= step - 3:
            for head in groups[step - 3]:
                mix(head, *found[head])


def key_table(views, rows, tok_dev):
    columns = []
    for half in range(2):
        for _, _, partner, across, slots in views:
            for k in slots:
                for turn in (0, 2):
                    place = [row - 2 * k * tok_dev for row in range(rows)]
                    columns += [(p, partner, turn, half, across) for p in place]
    return np.array(columns, np.int32).T


def attend(doc_lengths, queries, w_key, w_value, pieces, views, group, state, last):
    heads, rows, width = queries.shape
    first = state is None
    table = jnp.asarray(key_table(views, 16, rows))
    count = table.shape[1]
    vmem = pl.BlockSpec(memory_space=pltpu.VMEM)
    args = [queries, table, w_key, w_value, *pieces]
    if not first:
        args += list(state)
    args = [slow(doc_lengths), *[fast(a) for a in args]]
    if last:
        out_shape = jax.ShapeDtypeStruct((rows, heads * VD), jnp.bfloat16)
        out_specs = vmem
    else:
        out_shape = [pltpu.VMEM((heads, rows, VD), jnp.float32)] * 3
        out_specs = [vmem] * 3

    def kernel(*refs):
        attend_kernel(views, group, first, last, *refs)

    return pl.pallas_call(
        kernel,
        in_specs=[pl.BlockSpec(memory_space=pltpu.SMEM)] + [vmem] * (len(args) - 1),
        out_specs=out_specs,
        out_shape=out_shape,
        scratch_shapes=[
            pltpu.VMEM((count, KL), jnp.bfloat16),
            pltpu.VMEM((count, LANES), jnp.bfloat16),
            pltpu.VMEM((rows, count), jnp.float32),
            pltpu.VMEM((KL + LANES, count), jnp.bfloat16),
            pltpu.VMEM((heads * ND, count), jnp.bfloat16),
            pltpu.VMEM((count, heads * VD), jnp.bfloat16),
            pltpu.VMEM((heads, rows, count), jnp.float32),
            pltpu.VMEM((heads, rows, count), jnp.bfloat16),
        ],
        compiler_params=LARGE,
    )(*args)


def body(q_latent, q_gain, kv_cache, kv_gain, w_query, w_kv, doc_lengths):
    ctx_size, head_size = lax.axis_size("ctx"), lax.axis_size("head")
    chips, ys = ctx_size // 2, head_size // 2
    tok_dev = q_latent.shape[0] * head_size
    heads_here = w_query.shape[1] // (ND + RD)
    ctx, head = lax.axis_index("ctx"), lax.axis_index("head")
    vmem = pl.BlockSpec(memory_space=pltpu.VMEM)

    swap = [(n, n ^ 1) for n in range(ctx_size)]
    across_x = [(n, n ^ 1) for n in range(head_size)]

    def chip_shift(step):
        return [(2 * n + c, 2 * ((n + step) % chips) + c) for n in range(chips) for c in range(2)]

    apart = [
        ((2 * n + c) * head_size + h, (2 * n + c) * head_size + (h + 2 - 4 * c) % head_size)
        for n in range(chips)
        for c in range(2)
        for h in range(head_size)
    ]

    across_y = [(n, (n + ys) % head_size) for n in range(head_size)]

    size, q_width = q_latent.shape
    kv_width = kv_cache.shape[1]
    rows = pl.pallas_call(
        norm_kernel,
        out_shape=pltpu.VMEM((size, q_width + kv_width), jnp.bfloat16),
        compiler_params=SMALL,
    )(*[slow(a) for a in (q_latent, q_gain, kv_cache, kv_gain)])
    other = lax.ppermute(rows, "head", across_x)
    w_kv, rows = lax.optimization_barrier((w_kv, rows))
    w_key, w_value = pl.pallas_call(
        split_kernel,
        in_specs=[vmem],
        out_specs=[vmem] * 2,
        out_shape=[
            pltpu.VMEM((heads_here * ND, KL), jnp.bfloat16),
            pltpu.VMEM((KL, heads_here * VD), jnp.bfloat16),
        ],
        compiler_params=SMALL,
    )(fast(w_kv))
    both = pl.pallas_call(
        pair_kernel,
        in_specs=[vmem] * 3,
        out_specs=vmem,
        out_shape=pltpu.VMEM((size, 2 * rows.shape[1]), jnp.bfloat16),
        compiler_params=SMALL,
    )(fast(rows), fast(other), fast(w_key))
    opposite = lax.ppermute(both, "head", across_y)
    w_query, both = lax.optimization_barrier((w_query, both))
    w_query = pl.pallas_call(
        fetch_kernel,
        in_specs=[pl.BlockSpec(memory_space=pl.ANY)],
        out_specs=vmem,
        out_shape=pltpu.VMEM(w_query.shape, w_query.dtype),
        scratch_shapes=[pltpu.SemaphoreType.DMA],
        compiler_params=SMALL,
    )(slow(w_query))
    piece, q_set = pl.pallas_call(
        part_kernel,
        in_specs=[vmem] * 3,
        out_specs=[vmem] * 2,
        out_shape=[
            pltpu.VMEM((2 * size, 2 * kv_width), jnp.bfloat16),
            pltpu.VMEM((2 * size, 2 * q_width), jnp.bfloat16),
        ],
        compiler_params=SMALL,
    )(fast(both), fast(opposite), fast(w_query))
    coarse = [lax.ppermute(piece, "ctx", chip_shift(step)) for step in COARSE]
    set_shape = coarse[0].shape
    q_at = len(COARSE) * set_shape[1]
    coarse, bundle = pl.pallas_call(
        lambda *refs: bundle_kernel(len(COARSE), *refs),
        in_specs=[vmem] * (len(COARSE) + 1),
        out_specs=[vmem] * 2,
        out_shape=[
            pltpu.VMEM((len(COARSE) * set_shape[0], set_shape[1]), jnp.bfloat16),
            pltpu.VMEM((set_shape[0], q_at + q_set.shape[1]), jnp.bfloat16),
        ],
        compiler_params=SMALL,
    )(*[fast(a) for a in (*coarse, q_set)])
    later = lax.ppermute(coarse, "ctx", chip_shift(1))
    sooner = lax.ppermute(coarse, "ctx", chip_shift(-1))
    got = lax.ppermute(bundle, ("ctx", "head"), apart)
    coarse_swapped = lax.ppermute(coarse, "ctx", swap)

    (near,) = join([[later, sooner]])
    received = lax.ppermute(near, ("ctx", "head"), apart)
    near_swapped = lax.ppermute(near, "ctx", swap)
    got_swapped = lax.ppermute(got, "ctx", swap)

    queries = pl.pallas_call(
        lambda *refs: query_kernel(q_at, *refs),
        in_specs=[pl.BlockSpec(memory_space=pltpu.SMEM)] + [vmem] * 3,
        out_specs=vmem,
        out_shape=pltpu.VMEM((heads_here, tok_dev, 2 * LANES), jnp.bfloat16),
        scratch_shapes=[pltpu.VMEM((tok_dev, w_query.shape[0]), jnp.bfloat16)],
        compiler_params=SMALL,
    )(slow(doc_lengths), fast(q_set), fast(got), fast(w_query))

    def attend_to(pieces, views, group, state, last=False):
        return attend(doc_lengths, queries, w_key, w_value, pieces, views, group, state, last)

    near_slots = [*[k + 1 for k in COARSE], *[k - 1 for k in COARSE]]
    views = [(0, 0, 0, 0, COARSE), (1, 0, 0, 0, near_slots)]
    views += [(2, 0, 1, 0, COARSE), (3, 0, 1, 0, near_slots)]
    for partner in range(2):
        for n, k in enumerate(COARSE):
            views.append((4 + partner, n * set_shape[1], partner, 1, [k]))
    pieces = [coarse, near, coarse_swapped, near_swapped, got, got_swapped]
    state = attend_to(pieces, views, 2, None)
    received, state = lax.optimization_barrier((received, state))
    swapped = lax.ppermute(received, "ctx", swap)
    state = attend_to([received], [(0, 0, 0, 1, near_slots)], 1, state)
    return attend_to([swapped], [(0, 0, 1, 1, near_slots)], 1, state, last=True)


def solution(mesh):
    placed = (
        P(("ctx", "head"), None),
        P(),
        P(("ctx", "head"), None),
        P(),
        P(None, "head"),
        P(None, "head"),
        P(),
    )
    return jax.shard_map(
        body, mesh=mesh, in_specs=placed, out_specs=P("ctx", "head"), check_vma=False
    )
```

```python
import math

import jax
import jax.numpy as jnp
import numpy as np
from jax import lax
from jax.experimental import pallas as pl
from jax.experimental.pallas import tpu as pltpu
from jax.sharding import PartitionSpec as P

KL = 512
RD = 64
ND = 128
VD = 128
LANES = 128
EPSILON = 1e-06
MASKED = -1e30
FLOOR = -1e29
COARSE = (4, 1, 7)
SCORE_SCALE = math.log2(math.e) / math.sqrt(ND + RD)


SMALL = pltpu.CompilerParams(vmem_limit_bytes=12 * 2**20)
LARGE = pltpu.CompilerParams(vmem_limit_bytes=28 * 2**20)


def fast(array):
    return pltpu.with_memory_space_constraint(array, pltpu.VMEM)


def slow(array):
    return pltpu.with_memory_space_constraint(array, pltpu.HBM)


def here():
    ctx, head = lax.axis_index("ctx"), lax.axis_index("head")
    return ctx // 2, lax.rem(ctx, 2), head // 2, lax.rem(head, 2)


def scaled(values, gain):
    mean = jnp.mean(values * values, axis=-1, keepdims=True)
    return values * lax.rsqrt(mean + EPSILON) * gain


def norm_kernel(q_ref, q_gain_ref, kv_ref, kv_gain_ref, out_ref):
    latent = kv_ref[:, :KL].astype(jnp.float32)
    out_ref[:, :KL] = scaled(latent, kv_gain_ref[...][None, :]).astype(jnp.bfloat16)
    rows = q_ref[...].astype(jnp.float32)
    q_end = KL + rows.shape[1]
    out_ref[:, KL:q_end] = scaled(rows, q_gain_ref[...][None, :]).astype(jnp.bfloat16)
    out_ref[:, q_end:] = kv_ref[:, KL:]


def split_kernel(w_ref, key_ref, value_ref):
    for head in range(key_ref.shape[0] // ND):
        at = head * (ND + VD)
        key_ref[head * ND : (head + 1) * ND, :] = w_ref[:, at : at + ND].T
        value_ref[:, head * VD : (head + 1) * VD] = w_ref[:, at + ND : at + ND + VD]


def fetch_kernel(from_ref, to_ref, arrived):
    pltpu.async_copy(from_ref, to_ref, arrived).wait()


def pair_kernel(own_ref, other_ref, ready_ref, kv_ref, q_ref):
    q_end = own_ref.shape[1] - RD
    q_size = q_end - KL
    for n, ref in enumerate((own_ref, other_ref)):
        kv_ref[:, n * KL : (n + 1) * KL] = ref[:, :KL]
        q_ref[:, n * q_size : (n + 1) * q_size] = ref[:, KL:q_end]
    kv_ref[:, 2 * KL :] = jnp.concatenate([own_ref[:, q_end:], other_ref[:, q_end:]], axis=1)


def bundle_kernel(coarse_ref, q_own_ref, q_got_ref, q_ref, bundle_ref):
    size, width = q_ref.shape[0], coarse_ref.shape[1]
    n_parts = coarse_ref.shape[0] // size
    for n in range(n_parts):
        bundle_ref[:, n * width : (n + 1) * width] = coarse_ref[n * size : (n + 1) * size, :]
    for n, ref in enumerate((q_own_ref, q_got_ref)):
        rows = slice(n * ref.shape[0], (n + 1) * ref.shape[0])
        q_ref[rows, :] = ref[...]
        bundle_ref[rows, n_parts * width :] = ref[...]


def join_kernel(sizes, n_after, *refs):
    outs = refs[len(refs) - len(sizes) :]
    at = 0
    for size, out_ref in zip(sizes, outs):
        row = 0
        for ref in refs[at : at + size]:
            out_ref[row : row + ref.shape[0], :] = ref[...]
            row += ref.shape[0]
        at += size


def join(groups, after=()):
    sizes = [len(g) for g in groups]
    shapes = [
        pltpu.VMEM((sum(a.shape[0] for a in g), g[0].shape[1]), g[0].dtype)
        for g in groups
    ]
    arrays = [a for g in groups for a in g]
    vmem = pl.BlockSpec(memory_space=pltpu.VMEM)

    def kernel(*refs):
        join_kernel(sizes, len(after), *refs)

    return pl.pallas_call(
        kernel,
        in_specs=[vmem] * (len(arrays) + len(after)),
        out_specs=[vmem] * len(groups),
        out_shape=shapes,
        compiler_params=SMALL,
    )(*[fast(a) for a in (*arrays, *after)])


def document_start(position, lengths):
    start, end = jnp.zeros_like(position), 0
    for doc in range(lengths.shape[0]):
        end = end + lengths[doc]
        start = jnp.where(position >= end, end, start)
    return start


def query_kernel(q_at, lengths, own, got, w_ref, out_ref, rows_ref):
    chip, core, y, xh = here()
    width = rows_ref.shape[1]
    for base, ref, lane_at in ((y, own, 0), (y + jnp.where(core == 0, 3, 1), got, q_at)):
        for n in range(4):
            turn, half = n // 2, n % 2
            place = lax.rem(base + 2 * turn, 4) * 32 + lax.rem(xh + half, 2) * 16
            at = pl.multiple_of(place, 16)
            lanes = slice(lane_at + half * width, lane_at + (half + 1) * width)
            rows = ref[16 * turn : 16 * turn + 16, lanes]
            rows_ref[pl.ds(at, 16), :] = rows

    shape = (rows_ref.shape[0], LANES)
    lane = lax.broadcasted_iota(jnp.int32, shape, 1)
    position = (2 * chip + core) * shape[0] + lax.broadcasted_iota(jnp.int32, shape, 0)
    offset = (position - document_start(position, lengths)).astype(jnp.float32)
    freq_index = lax.rem(lane, RD // 2).astype(jnp.float32)
    angles = offset * jnp.exp(freq_index * (-2.0 * math.log(10000.0) / RD))
    cosine = jnp.where(lane < RD, jnp.cos(angles), 0.0)
    sine = jnp.sin(angles)
    sine = jnp.where(lane < RD // 2, -sine, jnp.where(lane < RD, sine, 0.0))

    def rotated(rope):
        turned = jnp.where(
            lane < RD // 2, pltpu.roll(rope, LANES - RD // 2, 1), pltpu.roll(rope, RD // 2, 1)
        )
        return rope * cosine + turned * sine

    pair_width = 2 * (ND + RD)
    for pair in range(w_ref.shape[1] // pair_width):
        w = w_ref[:, pair * pair_width : (pair + 1) * pair_width]
        made = jnp.dot(rows_ref[...], w, preferred_element_type=jnp.float32)
        out_ref[2 * pair, :, :ND] = made[:, :ND].astype(jnp.bfloat16)
        out_ref[2 * pair, :, ND:] = rotated(made[:, ND : ND + LANES]).astype(jnp.bfloat16)
        second = ND + RD
        out_ref[2 * pair + 1, :, :ND] = made[:, second : second + ND].astype(jnp.bfloat16)
        rope = pltpu.roll(made[:, second + RD : second + RD + LANES], RD, 1)
        out_ref[2 * pair + 1, :, ND:] = rotated(rope).astype(jnp.bfloat16)


def attend_kernel(views, group, first, last, *refs):
    lengths, q_ref, table_ref, w_key_ref, w_value_ref = refs[:5]
    at = 5 + 1 + max(view[0] for view in views)
    pieces = refs[5:at]
    if not first:
        max_in, sum_in, acc_in = refs[at : at + 3]
        at += 3
    if last:
        (out_ref,) = refs[at : at + 1]
        at += 1
    else:
        max_out, sum_out, acc_out = refs[at : at + 3]
        at += 3
    rows_ref, rope_ref, bias_ref, turned_ref, key_ref, value_ref, score_ref, weight_ref = refs[at : at + 8]
    if last:
        made_ref, gone = refs[at + 8 :]
    heads = q_ref.shape[0]
    tok_dev, n_keys = bias_ref.shape

    row = 0
    for piece, lane_at, *_ in views:
        ref = pieces[piece]
        size = ref.shape[0]
        rope = ref[:, lane_at + 2 * KL : lane_at + 2 * (KL + RD)]
        turned = jnp.concatenate([rope[:, RD:], rope[:, :RD]], axis=1)
        for half in range(2):
            to = slice(row + half * (n_keys // 2), row + half * (n_keys // 2) + size)
            rows_ref[to, :] = ref[:, lane_at + half * KL : lane_at + (half + 1) * KL]
            rope_ref[to, :] = turned if half else rope
        row += size

    chip, core, y, xh = here()
    query_pos = (2 * chip + core) * tok_dev + lax.broadcasted_iota(jnp.int32, (tok_dev, 1), 0)
    query_start = document_start(query_pos, lengths)
    place, partner, turn, half, across = [table_ref[n : n + 1, :] for n in range(5)]
    holder = lax.rem(core + partner, 2)
    ys = lax.rem(y + turn + across * (3 - 2 * holder), 4)
    xs = lax.rem(xh + half, 2)
    key_pos = place + (2 * chip + holder) * tok_dev + ys * 32 + xs * 16
    allowed = (key_pos <= query_pos) & (key_pos >= query_start)
    bias_ref[...] = jnp.where(allowed, 0.0, MASKED)

    turned_ref[:KL, :] = rows_ref[...].T
    turned_ref[KL:, :] = rope_ref[...].T

    def expand(pair):
        some = slice(pair * 2 * ND, (pair + 1) * 2 * ND)
        keys = jnp.dot(w_key_ref[some, :], turned_ref[:KL, :], preferred_element_type=jnp.float32)
        key_ref[some, :] = keys.astype(jnp.bfloat16)
        values = jnp.dot(rows_ref[...], w_value_ref[:, some], preferred_element_type=jnp.float32)
        value_ref[:, some] = values.astype(jnp.bfloat16)

    def score(head):
        keys = [key_ref[head * ND : (head + 1) * ND, :], turned_ref[KL:, :]]
        keys = jnp.concatenate(keys, axis=0)
        scores = jnp.dot(q_ref[head], keys, preferred_element_type=jnp.float32)
        score_ref[head] = scores * SCORE_SCALE + bias_ref[...]

    def weigh(head):
        scores = score_ref[head]
        top = jnp.max(scores, axis=1, keepdims=True)
        old_max = FLOOR if first else max_in[head][:, :1]
        new_max = jnp.maximum(top, old_max)
        weights = jnp.exp2(scores - new_max)
        total = jnp.sum(weights, axis=1, keepdims=True)
        weight_ref[head] = weights.astype(jnp.bfloat16)
        if first:
            return new_max, total, None
        faded = jnp.exp2(old_max - new_max)
        return new_max, total + faded * sum_in[head][:, :1], faded

    def mix(head, new_max, total, faded):
        values = value_ref[:, head * VD : (head + 1) * VD]
        mixed = jnp.dot(weight_ref[head], values, preferred_element_type=jnp.float32)
        if not first:
            mixed = mixed + faded * acc_in[head]
        if last:
            made_ref[:, head * VD : (head + 1) * VD] = (mixed * (1.0 / total)).astype(jnp.bfloat16)
            if head % 2 == 1:
                copies[head // 2].start()
        else:
            max_out[head] = jnp.broadcast_to(new_max, mixed.shape)
            sum_out[head] = jnp.broadcast_to(total, mixed.shape)
            acc_out[head] = mixed

    copies = []
    for pair in range(heads // 2 if last else 0):
        some = slice(pair * 2 * VD, (pair + 1) * 2 * VD)
        copy = pltpu.make_async_copy(made_ref.at[:, some], out_ref.at[:, some], gone.at[pair])
        copies.append(copy)
    groups = [range(low, low + group) for low in range(0, heads, group)]
    found = {}
    for step in range(len(groups) + 3):
        if step < len(groups):
            for head in groups[step]:
                if head % 2 == 0:
                    expand(head // 2)
        if 0 <= step - 1 < len(groups):
            for head in groups[step - 1]:
                score(head)
        if 0 <= step - 2 < len(groups):
            for head in groups[step - 2]:
                found[head] = weigh(head)
        if 0 <= step - 3:
            for head in groups[step - 3]:
                mix(head, *found[head])
    for copy in copies:
        copy.wait()


def key_table(views, rows, tok_dev):
    columns = []
    for half in range(2):
        for _, _, partner, across, slots in views:
            for k in slots:
                for turn in (0, 2):
                    place = [row - 2 * k * tok_dev for row in range(rows)]
                    columns += [(p, partner, turn, half, across) for p in place]
    return np.array(columns, np.int32).T


def attend(doc_lengths, queries, w_key, w_value, pieces, views, group, state, last):
    heads, rows, width = queries.shape
    first = state is None
    table = jnp.asarray(key_table(views, 16, rows))
    count = table.shape[1]
    vmem = pl.BlockSpec(memory_space=pltpu.VMEM)
    args = [queries, table, w_key, w_value, *pieces]
    if not first:
        args += list(state)
    args = [slow(doc_lengths), *[fast(a) for a in args]]
    if last:
        out_shape = jax.ShapeDtypeStruct((rows, heads * VD), jnp.bfloat16)
        out_specs = pl.BlockSpec(memory_space=pl.ANY)
        leaving = [
            pltpu.VMEM((rows, heads * VD), jnp.bfloat16),
            pltpu.SemaphoreType.DMA((heads // 2,)),
        ]
    else:
        leaving = []
        out_shape = [pltpu.VMEM((heads, rows, VD), jnp.float32)] * 3
        out_specs = [vmem] * 3

    def kernel(*refs):
        attend_kernel(views, group, first, last, *refs)

    return pl.pallas_call(
        kernel,
        in_specs=[pl.BlockSpec(memory_space=pltpu.SMEM)] + [vmem] * (len(args) - 1),
        out_specs=out_specs,
        out_shape=out_shape,
        scratch_shapes=[
            pltpu.VMEM((count, KL), jnp.bfloat16),
            pltpu.VMEM((count, LANES), jnp.bfloat16),
            pltpu.VMEM((rows, count), jnp.float32),
            pltpu.VMEM((KL + LANES, count), jnp.bfloat16),
            pltpu.VMEM((heads * ND, count), jnp.bfloat16),
            pltpu.VMEM((count, heads * VD), jnp.bfloat16),
            pltpu.VMEM((heads, rows, count), jnp.float32),
            pltpu.VMEM((heads, rows, count), jnp.bfloat16),
            *leaving,
        ],
        compiler_params=LARGE,
    )(*args)


def body(q_latent, q_gain, kv_cache, kv_gain, w_query, w_kv, doc_lengths):
    ctx_size, head_size = lax.axis_size("ctx"), lax.axis_size("head")
    chips, ys = ctx_size // 2, head_size // 2
    tok_dev = q_latent.shape[0] * head_size
    heads_here = w_query.shape[1] // (ND + RD)
    ctx, head = lax.axis_index("ctx"), lax.axis_index("head")
    vmem = pl.BlockSpec(memory_space=pltpu.VMEM)

    swap = [(n, n ^ 1) for n in range(ctx_size)]
    across_x = [(n, n ^ 1) for n in range(head_size)]

    def chip_shift(step):
        return [(2 * n + c, 2 * ((n + step) % chips) + c) for n in range(chips) for c in range(2)]

    apart = [
        ((2 * n + c) * head_size + h, (2 * n + c) * head_size + (h + 2 - 4 * c) % head_size)
        for n in range(chips)
        for c in range(2)
        for h in range(head_size)
    ]

    across_y = [(n, (n + ys) % head_size) for n in range(head_size)]

    size, q_width = q_latent.shape
    kv_width = kv_cache.shape[1]
    rows = pl.pallas_call(
        norm_kernel,
        out_shape=pltpu.VMEM((size, q_width + kv_width), jnp.bfloat16),
        compiler_params=SMALL,
    )(*[slow(a) for a in (q_latent, q_gain, kv_cache, kv_gain)])
    other = lax.ppermute(rows, "head", across_x)
    w_kv, rows = lax.optimization_barrier((w_kv, rows))
    w_key, w_value = pl.pallas_call(
        split_kernel,
        in_specs=[vmem],
        out_specs=[vmem] * 2,
        out_shape=[
            pltpu.VMEM((heads_here * ND, KL), jnp.bfloat16),
            pltpu.VMEM((KL, heads_here * VD), jnp.bfloat16),
        ],
        compiler_params=SMALL,
    )(fast(w_kv))
    piece, q_pair = pl.pallas_call(
        pair_kernel,
        in_specs=[vmem] * 3,
        out_specs=[vmem] * 2,
        out_shape=[
            pltpu.VMEM((size, 2 * kv_width), jnp.bfloat16),
            pltpu.VMEM((size, 2 * q_width), jnp.bfloat16),
        ],
        compiler_params=SMALL,
    )(fast(rows), fast(other), fast(w_key))
    opposite = lax.ppermute(piece, "head", across_y)
    w_query, piece = lax.optimization_barrier((w_query, piece))
    w_query = pl.pallas_call(
        fetch_kernel,
        in_specs=[pl.BlockSpec(memory_space=pl.ANY)],
        out_specs=vmem,
        out_shape=pltpu.VMEM(w_query.shape, w_query.dtype),
        scratch_shapes=[pltpu.SemaphoreType.DMA],
        compiler_params=SMALL,
    )(slow(w_query))
    (piece,) = join([[piece, opposite]], after=[w_query])
    q_opposite = lax.ppermute(q_pair, "head", across_y)
    coarse = [lax.ppermute(piece, "ctx", chip_shift(step)) for step in COARSE]

    set_shape = coarse[0].shape
    q_at = len(COARSE) * set_shape[1]
    (coarse,) = join([coarse])
    q_set, bundle = pl.pallas_call(
        bundle_kernel,
        in_specs=[vmem] * 3,
        out_specs=[vmem] * 2,
        out_shape=[
            pltpu.VMEM((set_shape[0], q_pair.shape[1]), jnp.bfloat16),
            pltpu.VMEM((set_shape[0], q_at + q_pair.shape[1]), jnp.bfloat16),
        ],
        compiler_params=SMALL,
    )(*[fast(a) for a in (coarse, q_pair, q_opposite)])
    later = lax.ppermute(coarse, "ctx", chip_shift(1))
    sooner = lax.ppermute(coarse, "ctx", chip_shift(-1))
    got = lax.ppermute(bundle, ("ctx", "head"), apart)
    coarse_swapped = lax.ppermute(coarse, "ctx", swap)

    queries = pl.pallas_call(
        lambda *refs: query_kernel(q_at, *refs),
        in_specs=[pl.BlockSpec(memory_space=pltpu.SMEM)] + [vmem] * 3,
        out_specs=vmem,
        out_shape=pltpu.VMEM((heads_here, tok_dev, 2 * LANES), jnp.bfloat16),
        scratch_shapes=[pltpu.VMEM((tok_dev, w_query.shape[0]), jnp.bfloat16)],
        compiler_params=SMALL,
    )(slow(doc_lengths), fast(q_set), fast(got), fast(w_query))

    (near,) = join([[later, sooner]], after=[queries])
    received = lax.ppermute(near, ("ctx", "head"), apart)
    near_swapped = lax.ppermute(near, "ctx", swap)
    got_swapped = lax.ppermute(got, "ctx", swap)

    def attend_to(pieces, views, group, state, last=False):
        return attend(doc_lengths, queries, w_key, w_value, pieces, views, group, state, last)

    near_slots = [*[k + 1 for k in COARSE], *[k - 1 for k in COARSE]]
    views = [(0, 0, 0, 0, COARSE), (1, 0, 0, 0, near_slots)]
    views += [(2, 0, 1, 0, COARSE), (3, 0, 1, 0, near_slots)]
    for partner in range(2):
        for n, k in enumerate(COARSE):
            views.append((4 + partner, n * set_shape[1], partner, 1, [k]))
    pieces = [coarse, near, coarse_swapped, near_swapped, got, got_swapped]
    state = attend_to(pieces, views, 2, None)
    received, state = lax.optimization_barrier((received, state))
    swapped = lax.ppermute(received, "ctx", swap)
    state = attend_to([received], [(0, 0, 0, 1, near_slots)], 1, state)
    return attend_to([swapped], [(0, 0, 1, 1, near_slots)], 1, state, last=True)


def solution(mesh):
    placed = (
        P(("ctx", "head"), None),
        P(),
        P(("ctx", "head"), None),
        P(),
        P(None, "head"),
        P(None, "head"),
        P(),
    )
    return jax.shard_map(
        body, mesh=mesh, in_specs=placed, out_specs=P("ctx", "head"), check_vma=False
    )
```

```python
import math

import jax
import jax.numpy as jnp
import numpy as np
from jax import lax
from jax.experimental import pallas as pl
from jax.experimental.pallas import tpu as pltpu
from jax.sharding import PartitionSpec as P

KL = 512
RD = 64
ND = 128
VD = 128
LANES = 128
EPSILON = 1e-06
MASKED = -1e30
FLOOR = -1e29
COARSE = (7, 1, 4)
SCORE_SCALE = math.log2(math.e) / math.sqrt(ND + RD)


SMALL = pltpu.CompilerParams(vmem_limit_bytes=12 * 2**20)
LARGE = pltpu.CompilerParams(vmem_limit_bytes=28 * 2**20)


def fast(array):
    return pltpu.with_memory_space_constraint(array, pltpu.VMEM)


def slow(array):
    return pltpu.with_memory_space_constraint(array, pltpu.HBM)


def here():
    ctx, head = lax.axis_index("ctx"), lax.axis_index("head")
    return ctx // 2, lax.rem(ctx, 2), head // 2, lax.rem(head, 2)


def scaled(values, gain):
    mean = jnp.mean(values * values, axis=-1, keepdims=True)
    return values * lax.rsqrt(mean + EPSILON) * gain


def norm_kernel(q_ref, q_gain_ref, kv_ref, kv_gain_ref, out_ref):
    latent = kv_ref[:, :KL].astype(jnp.float32)
    out_ref[:, :KL] = scaled(latent, kv_gain_ref[...][None, :]).astype(jnp.bfloat16)
    rows = q_ref[...].astype(jnp.float32)
    q_end = KL + rows.shape[1]
    out_ref[:, KL:q_end] = scaled(rows, q_gain_ref[...][None, :]).astype(jnp.bfloat16)
    out_ref[:, q_end:] = kv_ref[:, KL:]


def split_kernel(w_ref, key_ref, value_ref):
    for head in range(key_ref.shape[0] // ND):
        at = head * (ND + VD)
        key_ref[head * ND : (head + 1) * ND, :] = w_ref[:, at : at + ND].T
        value_ref[:, head * VD : (head + 1) * VD] = w_ref[:, at + ND : at + ND + VD]


def fetch_kernel(from_ref, to_ref, arrived):
    pltpu.async_copy(from_ref, to_ref, arrived).wait()


def pair_kernel(own_ref, other_ref, ready_ref, kv_ref, q_ref):
    q_end = own_ref.shape[1] - RD
    q_size = q_end - KL
    for n, ref in enumerate((own_ref, other_ref)):
        kv_ref[:, n * KL : (n + 1) * KL] = ref[:, :KL]
        q_ref[:, n * q_size : (n + 1) * q_size] = ref[:, KL:q_end]
    kv_ref[:, 2 * KL :] = jnp.concatenate([own_ref[:, q_end:], other_ref[:, q_end:]], axis=1)


def join_kernel(sizes, n_after, *refs):
    outs = refs[len(refs) - len(sizes) :]
    at = 0
    for size, out_ref in zip(sizes, outs):
        row = 0
        for ref in refs[at : at + size]:
            out_ref[row : row + ref.shape[0], :] = ref[...]
            row += ref.shape[0]
        at += size


def join(groups, after=()):
    sizes = [len(g) for g in groups]
    shapes = [
        pltpu.VMEM((sum(a.shape[0] for a in g), g[0].shape[1]), g[0].dtype)
        for g in groups
    ]
    arrays = [a for g in groups for a in g]
    vmem = pl.BlockSpec(memory_space=pltpu.VMEM)

    def kernel(*refs):
        join_kernel(sizes, len(after), *refs)

    return pl.pallas_call(
        kernel,
        in_specs=[vmem] * (len(arrays) + len(after)),
        out_specs=[vmem] * len(groups),
        out_shape=shapes,
        compiler_params=SMALL,
    )(*[fast(a) for a in (*arrays, *after)])


def document_start(position, lengths):
    start, end = jnp.zeros_like(position), 0
    for doc in range(lengths.shape[0]):
        end = end + lengths[doc]
        start = jnp.where(position >= end, end, start)
    return start


def query_kernel(lengths, own, got, w_ref, out_ref, rows_ref):
    chip, core, y, xh = here()
    width = rows_ref.shape[1]
    for base, ref in ((y, own), (y + jnp.where(core == 0, 3, 1), got)):
        for n in range(4):
            turn, half = n // 2, n % 2
            place = lax.rem(base + 2 * turn, 4) * 32 + lax.rem(xh + half, 2) * 16
            at = pl.multiple_of(place, 16)
            rows = ref[16 * turn : 16 * turn + 16, half * width : (half + 1) * width]
            rows_ref[pl.ds(at, 16), :] = rows

    shape = (rows_ref.shape[0], LANES)
    lane = lax.broadcasted_iota(jnp.int32, shape, 1)
    position = (2 * chip + core) * shape[0] + lax.broadcasted_iota(jnp.int32, shape, 0)
    offset = (position - document_start(position, lengths)).astype(jnp.float32)
    freq_index = lax.rem(lane, RD // 2).astype(jnp.float32)
    angles = offset * jnp.exp(freq_index * (-2.0 * math.log(10000.0) / RD))
    cosine = jnp.where(lane < RD, jnp.cos(angles), 0.0)
    sine = jnp.sin(angles)
    sine = jnp.where(lane < RD // 2, -sine, jnp.where(lane < RD, sine, 0.0))

    def rotated(rope):
        turned = jnp.where(
            lane < RD // 2, pltpu.roll(rope, LANES - RD // 2, 1), pltpu.roll(rope, RD // 2, 1)
        )
        return rope * cosine + turned * sine

    pair_width = 2 * (ND + RD)
    for pair in range(w_ref.shape[1] // pair_width):
        w = w_ref[:, pair * pair_width : (pair + 1) * pair_width]
        made = jnp.dot(rows_ref[...], w, preferred_element_type=jnp.float32)
        out_ref[2 * pair, :, :ND] = made[:, :ND].astype(jnp.bfloat16)
        out_ref[2 * pair, :, ND:] = rotated(made[:, ND : ND + LANES]).astype(jnp.bfloat16)
        second = ND + RD
        out_ref[2 * pair + 1, :, :ND] = made[:, second : second + ND].astype(jnp.bfloat16)
        rope = pltpu.roll(made[:, second + RD : second + RD + LANES], RD, 1)
        out_ref[2 * pair + 1, :, ND:] = rotated(rope).astype(jnp.bfloat16)


def attend_kernel(views, group, first, last, *refs):
    lengths, q_ref, table_ref, w_key_ref, w_value_ref = refs[:5]
    at = 5 + 1 + max(view[0] for view in views)
    pieces = refs[5:at]
    if not first:
        max_in, sum_in, acc_in = refs[at : at + 3]
        at += 3
    if last:
        (out_ref,) = refs[at : at + 1]
        at += 1
    else:
        max_out, sum_out, acc_out = refs[at : at + 3]
        at += 3
    rows_ref, rope_ref, bias_ref, turned_ref, key_ref, value_ref, score_ref, weight_ref = refs[at : at + 8]
    if last:
        made_ref, gone = refs[at + 8 :]
    heads = q_ref.shape[0]
    tok_dev, n_keys = bias_ref.shape

    row = 0
    for piece, lane_at, *_ in views:
        ref = pieces[piece]
        size = ref.shape[0]
        rope = ref[:, lane_at + 2 * KL : lane_at + 2 * (KL + RD)]
        turned = jnp.concatenate([rope[:, RD:], rope[:, :RD]], axis=1)
        for half in range(2):
            to = slice(row + half * (n_keys // 2), row + half * (n_keys // 2) + size)
            rows_ref[to, :] = ref[:, lane_at + half * KL : lane_at + (half + 1) * KL]
            rope_ref[to, :] = turned if half else rope
        row += size

    chip, core, y, xh = here()
    query_pos = (2 * chip + core) * tok_dev + lax.broadcasted_iota(jnp.int32, (tok_dev, 1), 0)
    query_start = document_start(query_pos, lengths)
    place, partner, turn, half, across = [table_ref[n : n + 1, :] for n in range(5)]
    holder = lax.rem(core + partner, 2)
    ys = lax.rem(y + turn + across * (3 - 2 * holder), 4)
    xs = lax.rem(xh + half, 2)
    key_pos = place + (2 * chip + holder) * tok_dev + ys * 32 + xs * 16
    allowed = (key_pos <= query_pos) & (key_pos >= query_start)
    bias_ref[...] = jnp.where(allowed, 0.0, MASKED)

    turned_ref[:KL, :] = rows_ref[...].T
    turned_ref[KL:, :] = rope_ref[...].T

    def expand(pair):
        some = slice(pair * 2 * ND, (pair + 1) * 2 * ND)
        keys = jnp.dot(w_key_ref[some, :], turned_ref[:KL, :], preferred_element_type=jnp.float32)
        key_ref[some, :] = keys.astype(jnp.bfloat16)
        values = jnp.dot(rows_ref[...], w_value_ref[:, some], preferred_element_type=jnp.float32)
        value_ref[:, some] = values.astype(jnp.bfloat16)

    def score(head):
        keys = [key_ref[head * ND : (head + 1) * ND, :], turned_ref[KL:, :]]
        keys = jnp.concatenate(keys, axis=0)
        scores = jnp.dot(q_ref[head], keys, preferred_element_type=jnp.float32)
        score_ref[head] = scores * SCORE_SCALE + bias_ref[...]

    def weigh(head):
        scores = score_ref[head]
        top = jnp.max(scores, axis=1, keepdims=True)
        old_max = FLOOR if first else max_in[head][:, :1]
        new_max = jnp.maximum(top, old_max)
        weights = jnp.exp2(scores - new_max)
        total = jnp.sum(weights, axis=1, keepdims=True)
        weight_ref[head] = weights.astype(jnp.bfloat16)
        if first:
            return new_max, total, None
        faded = jnp.exp2(old_max - new_max)
        return new_max, total + faded * sum_in[head][:, :1], faded

    def mix(head, new_max, total, faded):
        values = value_ref[:, head * VD : (head + 1) * VD]
        mixed = jnp.dot(weight_ref[head], values, preferred_element_type=jnp.float32)
        if not first:
            mixed = mixed + faded * acc_in[head]
        if last:
            made_ref[:, head * VD : (head + 1) * VD] = (mixed * (1.0 / total)).astype(jnp.bfloat16)
            if head % 2 == 1:
                copies[head // 2].start()
        else:
            max_out[head] = jnp.broadcast_to(new_max, mixed.shape)
            sum_out[head] = jnp.broadcast_to(total, mixed.shape)
            acc_out[head] = mixed

    copies = []
    for pair in range(heads // 2 if last else 0):
        some = slice(pair * 2 * VD, (pair + 1) * 2 * VD)
        copy = pltpu.make_async_copy(made_ref.at[:, some], out_ref.at[:, some], gone.at[pair])
        copies.append(copy)
    groups = [range(low, low + group) for low in range(0, heads, group)]
    found = {}
    for step in range(len(groups) + 3):
        if step < len(groups):
            for head in groups[step]:
                if head % 2 == 0:
                    expand(head // 2)
        if 0 <= step - 1 < len(groups):
            for head in groups[step - 1]:
                score(head)
        if 0 <= step - 2 < len(groups):
            for head in groups[step - 2]:
                found[head] = weigh(head)
        if 0 <= step - 3:
            for head in groups[step - 3]:
                mix(head, *found[head])
    for copy in copies:
        copy.wait()


def key_table(views, rows, tok_dev):
    columns = []
    for half in range(2):
        for _, _, partner, across, slots in views:
            for k in slots:
                for turn in (0, 2):
                    place = [row - 2 * k * tok_dev for row in range(rows)]
                    columns += [(p, partner, turn, half, across) for p in place]
    return np.array(columns, np.int32).T


def attend(doc_lengths, queries, w_key, w_value, pieces, views, group, state, last):
    heads, rows, width = queries.shape
    first = state is None
    table = jnp.asarray(key_table(views, 16, rows))
    count = table.shape[1]
    vmem = pl.BlockSpec(memory_space=pltpu.VMEM)
    args = [queries, table, w_key, w_value, *pieces]
    if not first:
        args += list(state)
    args = [slow(doc_lengths), *[fast(a) for a in args]]
    if last:
        out_shape = jax.ShapeDtypeStruct((rows, heads * VD), jnp.bfloat16)
        out_specs = pl.BlockSpec(memory_space=pl.ANY)
        leaving = [
            pltpu.VMEM((rows, heads * VD), jnp.bfloat16),
            pltpu.SemaphoreType.DMA((heads // 2,)),
        ]
    else:
        leaving = []
        out_shape = [pltpu.VMEM((heads, rows, VD), jnp.float32)] * 3
        out_specs = [vmem] * 3

    def kernel(*refs):
        attend_kernel(views, group, first, last, *refs)

    return pl.pallas_call(
        kernel,
        in_specs=[pl.BlockSpec(memory_space=pltpu.SMEM)] + [vmem] * (len(args) - 1),
        out_specs=out_specs,
        out_shape=out_shape,
        scratch_shapes=[
            pltpu.VMEM((count, KL), jnp.bfloat16),
            pltpu.VMEM((count, LANES), jnp.bfloat16),
            pltpu.VMEM((rows, count), jnp.float32),
            pltpu.VMEM((KL + LANES, count), jnp.bfloat16),
            pltpu.VMEM((heads * ND, count), jnp.bfloat16),
            pltpu.VMEM((count, heads * VD), jnp.bfloat16),
            pltpu.VMEM((heads, rows, count), jnp.float32),
            pltpu.VMEM((heads, rows, count), jnp.bfloat16),
            *leaving,
        ],
        compiler_params=LARGE,
    )(*args)


def body(q_latent, q_gain, kv_cache, kv_gain, w_query, w_kv, doc_lengths):
    ctx_size, head_size = lax.axis_size("ctx"), lax.axis_size("head")
    chips, ys = ctx_size // 2, head_size // 2
    tok_dev = q_latent.shape[0] * head_size
    heads_here = w_query.shape[1] // (ND + RD)
    ctx, head = lax.axis_index("ctx"), lax.axis_index("head")
    vmem = pl.BlockSpec(memory_space=pltpu.VMEM)

    swap = [(n, n ^ 1) for n in range(ctx_size)]
    across_x = [(n, n ^ 1) for n in range(head_size)]

    def chip_shift(step):
        return [(2 * n + c, 2 * ((n + step) % chips) + c) for n in range(chips) for c in range(2)]

    apart = [
        ((2 * n + c) * head_size + h, (2 * n + c) * head_size + (h + 2 - 4 * c) % head_size)
        for n in range(chips)
        for c in range(2)
        for h in range(head_size)
    ]

    across_y = [(n, (n + ys) % head_size) for n in range(head_size)]

    size, q_width = q_latent.shape
    kv_width = kv_cache.shape[1]
    rows = pl.pallas_call(
        norm_kernel,
        out_shape=pltpu.VMEM((size, q_width + kv_width), jnp.bfloat16),
        compiler_params=SMALL,
    )(*[slow(a) for a in (q_latent, q_gain, kv_cache, kv_gain)])
    other = lax.ppermute(rows, "head", across_x)
    w_kv, rows = lax.optimization_barrier((w_kv, rows))
    w_key, w_value = pl.pallas_call(
        split_kernel,
        in_specs=[vmem],
        out_specs=[vmem] * 2,
        out_shape=[
            pltpu.VMEM((heads_here * ND, KL), jnp.bfloat16),
            pltpu.VMEM((KL, heads_here * VD), jnp.bfloat16),
        ],
        compiler_params=SMALL,
    )(fast(w_kv))
    piece, q_pair = pl.pallas_call(
        pair_kernel,
        in_specs=[vmem] * 3,
        out_specs=[vmem] * 2,
        out_shape=[
            pltpu.VMEM((size, 2 * kv_width), jnp.bfloat16),
            pltpu.VMEM((size, 2 * q_width), jnp.bfloat16),
        ],
        compiler_params=SMALL,
    )(fast(rows), fast(other), fast(w_key))
    opposite = lax.ppermute(piece, "head", across_y)
    (piece,) = join([[piece, opposite]])
    w_query, piece = lax.optimization_barrier((w_query, piece))
    w_query = pl.pallas_call(
        fetch_kernel,
        in_specs=[pl.BlockSpec(memory_space=pl.ANY)],
        out_specs=vmem,
        out_shape=pltpu.VMEM(w_query.shape, w_query.dtype),
        scratch_shapes=[pltpu.SemaphoreType.DMA],
        compiler_params=SMALL,
    )(slow(w_query))
    q_opposite = lax.ppermute(q_pair, "head", across_y)
    coarse = [lax.ppermute(piece, "ctx", chip_shift(step)) for step in COARSE]

    (coarse,) = join([coarse], after=[w_query])
    (q_set,) = join([[q_pair, q_opposite]], after=[coarse])
    coarse, q_set = lax.optimization_barrier((coarse, q_set))
    later = lax.ppermute(coarse, "ctx", chip_shift(1))
    sooner = lax.ppermute(coarse, "ctx", chip_shift(-1))
    q_got = lax.ppermute(q_set, ("ctx", "head"), apart)
    got = lax.ppermute(coarse, ("ctx", "head"), apart)
    coarse_swapped = lax.ppermute(coarse, "ctx", swap)

    queries = pl.pallas_call(
        query_kernel,
        in_specs=[pl.BlockSpec(memory_space=pltpu.SMEM)] + [vmem] * 3,
        out_specs=vmem,
        out_shape=pltpu.VMEM((heads_here, tok_dev, 2 * LANES), jnp.bfloat16),
        scratch_shapes=[pltpu.VMEM((tok_dev, w_query.shape[0]), jnp.bfloat16)],
        compiler_params=SMALL,
    )(slow(doc_lengths), fast(q_set), fast(q_got), fast(w_query))

    (near,) = join([[later, sooner]], after=[q_got])
    received = lax.ppermute(near, ("ctx", "head"), apart)
    near_swapped = lax.ppermute(near, "ctx", swap)
    got_swapped = lax.ppermute(got, "ctx", swap)

    def attend_to(pieces, views, group, state, last=False):
        return attend(doc_lengths, queries, w_key, w_value, pieces, views, group, state, last)

    near_slots = [*[k + 1 for k in COARSE], *[k - 1 for k in COARSE]]
    views = [(0, 0, 0, 0, COARSE), (1, 0, 0, 0, near_slots)]
    views += [(2, 0, 1, 0, COARSE), (3, 0, 1, 0, near_slots)]
    views += [(4, 0, 0, 1, COARSE), (5, 0, 1, 1, COARSE)]
    pieces = [coarse, near, coarse_swapped, near_swapped, got, got_swapped]
    state = attend_to(pieces, views, 2, None)
    received, state = lax.optimization_barrier((received, state))
    swapped = lax.ppermute(received, "ctx", swap)
    state = attend_to([received], [(0, 0, 0, 1, near_slots)], 1, state)
    return attend_to([swapped], [(0, 0, 1, 1, near_slots)], 1, state, last=True)


def solution(mesh):
    placed = (
        P(("ctx", "head"), None),
        P(),
        P(("ctx", "head"), None),
        P(),
        P(None, "head"),
        P(None, "head"),
        P(),
    )
    return jax.shard_map(
        body, mesh=mesh, in_specs=placed, out_specs=P("ctx", "head"), check_vma=False
    )
```

```python
import math

import jax
import jax.numpy as jnp
import numpy as np
from jax import lax
from jax.experimental import pallas as pl
from jax.experimental.pallas import tpu as pltpu
from jax.sharding import PartitionSpec as P

KL = 512
RD = 64
ND = 128
VD = 128
LANES = 128
EPSILON = 1e-06
MASKED = -1e30
FLOOR = -1e29
COARSE = (4, 1, 7)
SCORE_SCALE = math.log2(math.e) / math.sqrt(ND + RD)


SMALL = pltpu.CompilerParams(vmem_limit_bytes=12 * 2**20)
LARGE = pltpu.CompilerParams(vmem_limit_bytes=28 * 2**20)


def fast(array):
    return pltpu.with_memory_space_constraint(array, pltpu.VMEM)


def slow(array):
    return pltpu.with_memory_space_constraint(array, pltpu.HBM)


def here():
    ctx, head = lax.axis_index("ctx"), lax.axis_index("head")
    return ctx // 2, lax.rem(ctx, 2), head // 2, lax.rem(head, 2)


def scaled(values, gain):
    mean = jnp.mean(values * values, axis=-1, keepdims=True)
    return values * lax.rsqrt(mean + EPSILON) * gain


def norm_kernel(q_ref, q_gain_ref, kv_ref, kv_gain_ref, out_ref):
    latent = kv_ref[:, :KL].astype(jnp.float32)
    out_ref[:, :KL] = scaled(latent, kv_gain_ref[...][None, :]).astype(jnp.bfloat16)
    rows = q_ref[...].astype(jnp.float32)
    q_end = KL + rows.shape[1]
    out_ref[:, KL:q_end] = scaled(rows, q_gain_ref[...][None, :]).astype(jnp.bfloat16)
    out_ref[:, q_end:] = kv_ref[:, KL:]


def split_kernel(w_ref, key_ref, value_ref):
    for head in range(key_ref.shape[0] // ND):
        at = head * (ND + VD)
        key_ref[head * ND : (head + 1) * ND, :] = w_ref[:, at : at + ND].T
        value_ref[:, head * VD : (head + 1) * VD] = w_ref[:, at + ND : at + ND + VD]


def fetch_kernel(from_ref, to_ref, arrived):
    pltpu.async_copy(from_ref, to_ref, arrived).wait()


def pair_kernel(own_ref, other_ref, ready_ref, out_ref):
    q_end = own_ref.shape[1] - RD
    q_size = q_end - KL
    at = 2 * (KL + RD)
    for n, ref in enumerate((own_ref, other_ref)):
        out_ref[:, n * KL : (n + 1) * KL] = ref[:, :KL]
        out_ref[:, at + n * q_size : at + (n + 1) * q_size] = ref[:, KL:q_end]
    rope = jnp.concatenate([own_ref[:, q_end:], other_ref[:, q_end:]], axis=1)
    out_ref[:, 2 * KL : at] = rope


def part_kernel(own_ref, got_ref, ready_ref, kv_ref, q_ref):
    size, width = own_ref.shape[0], kv_ref.shape[1]
    for n, ref in enumerate((own_ref, got_ref)):
        kv_ref[n * size : (n + 1) * size, :] = ref[:, :width]
        q_ref[n * size : (n + 1) * size, :] = ref[:, width:]


def bundle_kernel(n_parts, *refs):
    *parts, q_ref, coarse_ref, bundle_ref = refs
    size, width = parts[0].shape
    for n, ref in enumerate(parts):
        coarse_ref[n * size : (n + 1) * size, :] = ref[...]
        bundle_ref[:, n * width : (n + 1) * width] = ref[...]
    bundle_ref[:, n_parts * width :] = q_ref[...]


def join_kernel(sizes, n_after, *refs):
    outs = refs[len(refs) - len(sizes) :]
    at = 0
    for size, out_ref in zip(sizes, outs):
        row = 0
        for ref in refs[at : at + size]:
            out_ref[row : row + ref.shape[0], :] = ref[...]
            row += ref.shape[0]
        at += size


def join(groups, after=()):
    sizes = [len(g) for g in groups]
    shapes = [
        pltpu.VMEM((sum(a.shape[0] for a in g), g[0].shape[1]), g[0].dtype)
        for g in groups
    ]
    arrays = [a for g in groups for a in g]
    vmem = pl.BlockSpec(memory_space=pltpu.VMEM)

    def kernel(*refs):
        join_kernel(sizes, len(after), *refs)

    return pl.pallas_call(
        kernel,
        in_specs=[vmem] * (len(arrays) + len(after)),
        out_specs=[vmem] * len(groups),
        out_shape=shapes,
        compiler_params=SMALL,
    )(*[fast(a) for a in (*arrays, *after)])


def document_start(position, lengths):
    start, end = jnp.zeros_like(position), 0
    for doc in range(lengths.shape[0]):
        end = end + lengths[doc]
        start = jnp.where(position >= end, end, start)
    return start


def query_kernel(q_at, lengths, own, got, w_ref, out_ref, rows_ref):
    chip, core, y, xh = here()
    width = rows_ref.shape[1]
    for base, ref, lane_at in ((y, own, 0), (y + jnp.where(core == 0, 3, 1), got, q_at)):
        for n in range(4):
            turn, half = n // 2, n % 2
            place = lax.rem(base + 2 * turn, 4) * 32 + lax.rem(xh + half, 2) * 16
            at = pl.multiple_of(place, 16)
            lanes = slice(lane_at + half * width, lane_at + (half + 1) * width)
            rows = ref[16 * turn : 16 * turn + 16, lanes]
            rows_ref[pl.ds(at, 16), :] = rows

    shape = (rows_ref.shape[0], LANES)
    lane = lax.broadcasted_iota(jnp.int32, shape, 1)
    position = (2 * chip + core) * shape[0] + lax.broadcasted_iota(jnp.int32, shape, 0)
    offset = (position - document_start(position, lengths)).astype(jnp.float32)
    freq_index = lax.rem(lane, RD // 2).astype(jnp.float32)
    angles = offset * jnp.exp(freq_index * (-2.0 * math.log(10000.0) / RD))
    cosine = jnp.where(lane < RD, jnp.cos(angles), 0.0)
    sine = jnp.sin(angles)
    sine = jnp.where(lane < RD // 2, -sine, jnp.where(lane < RD, sine, 0.0))

    def rotated(rope):
        turned = jnp.where(
            lane < RD // 2, pltpu.roll(rope, LANES - RD // 2, 1), pltpu.roll(rope, RD // 2, 1)
        )
        return rope * cosine + turned * sine

    pair_width = 2 * (ND + RD)
    for pair in range(w_ref.shape[1] // pair_width):
        w = w_ref[:, pair * pair_width : (pair + 1) * pair_width]
        made = jnp.dot(rows_ref[...], w, preferred_element_type=jnp.float32)
        out_ref[2 * pair, :, :ND] = made[:, :ND].astype(jnp.bfloat16)
        out_ref[2 * pair, :, ND:] = rotated(made[:, ND : ND + LANES]).astype(jnp.bfloat16)
        second = ND + RD
        out_ref[2 * pair + 1, :, :ND] = made[:, second : second + ND].astype(jnp.bfloat16)
        rope = pltpu.roll(made[:, second + RD : second + RD + LANES], RD, 1)
        out_ref[2 * pair + 1, :, ND:] = rotated(rope).astype(jnp.bfloat16)


def attend_kernel(views, group, first, last, *refs):
    lengths, q_ref, table_ref, w_key_ref, w_value_ref = refs[:5]
    at = 5 + 1 + max(view[0] for view in views)
    pieces = refs[5:at]
    if not first:
        max_in, sum_in, acc_in = refs[at : at + 3]
        at += 3
    if last:
        (out_ref,) = refs[at : at + 1]
        at += 1
    else:
        max_out, sum_out, acc_out = refs[at : at + 3]
        at += 3
    rows_ref, rope_ref, bias_ref, turned_ref, key_ref, value_ref, score_ref, weight_ref = refs[at:]
    heads = q_ref.shape[0]
    tok_dev, n_keys = bias_ref.shape

    row = 0
    for piece, lane_at, *_ in views:
        ref = pieces[piece]
        size = ref.shape[0]
        rope = ref[:, lane_at + 2 * KL : lane_at + 2 * (KL + RD)]
        turned = jnp.concatenate([rope[:, RD:], rope[:, :RD]], axis=1)
        for half in range(2):
            to = slice(row + half * (n_keys // 2), row + half * (n_keys // 2) + size)
            rows_ref[to, :] = ref[:, lane_at + half * KL : lane_at + (half + 1) * KL]
            rope_ref[to, :] = turned if half else rope
        row += size

    chip, core, y, xh = here()
    query_pos = (2 * chip + core) * tok_dev + lax.broadcasted_iota(jnp.int32, (tok_dev, 1), 0)
    query_start = document_start(query_pos, lengths)
    place, partner, turn, half, across = [table_ref[n : n + 1, :] for n in range(5)]
    holder = lax.rem(core + partner, 2)
    ys = lax.rem(y + turn + across * (3 - 2 * holder), 4)
    xs = lax.rem(xh + half, 2)
    key_pos = place + (2 * chip + holder) * tok_dev + ys * 32 + xs * 16
    allowed = (key_pos <= query_pos) & (key_pos >= query_start)
    bias_ref[...] = jnp.where(allowed, 0.0, MASKED)

    turned_ref[:KL, :] = rows_ref[...].T
    turned_ref[KL:, :] = rope_ref[...].T

    def expand(pair):
        some = slice(pair * 2 * ND, (pair + 1) * 2 * ND)
        keys = jnp.dot(w_key_ref[some, :], turned_ref[:KL, :], preferred_element_type=jnp.float32)
        key_ref[some, :] = keys.astype(jnp.bfloat16)
        values = jnp.dot(rows_ref[...], w_value_ref[:, some], preferred_element_type=jnp.float32)
        value_ref[:, some] = values.astype(jnp.bfloat16)

    def score(head):
        keys = [key_ref[head * ND : (head + 1) * ND, :], turned_ref[KL:, :]]
        keys = jnp.concatenate(keys, axis=0)
        scores = jnp.dot(q_ref[head], keys, preferred_element_type=jnp.float32)
        score_ref[head] = scores * SCORE_SCALE + bias_ref[...]

    def weigh(head):
        scores = score_ref[head]
        top = jnp.broadcast_to(jnp.max(scores, axis=1, keepdims=True), (tok_dev, LANES))
        old_max = FLOOR if first else max_in[head]
        new_max = jnp.maximum(top, old_max)
        weights = jnp.exp2(scores - jnp.concatenate([new_max] * (n_keys // LANES), axis=1))
        total = jnp.broadcast_to(jnp.sum(weights, axis=1, keepdims=True), (tok_dev, LANES))
        weight_ref[head] = weights.astype(jnp.bfloat16)
        if not last:
            max_out[head] = new_max
        if first:
            sum_out[head] = total
            return total, None
        faded = jnp.exp2(old_max - new_max)
        total = total + faded * sum_in[head]
        if not last:
            sum_out[head] = total
        return total, faded

    def mix(head, total, faded):
        values = value_ref[:, head * VD : (head + 1) * VD]
        mixed = jnp.dot(weight_ref[head], values, preferred_element_type=jnp.float32)
        if not first:
            mixed = mixed + faded * acc_in[head]
        if last:
            out_ref[:, head * VD : (head + 1) * VD] = (mixed * (1.0 / total)).astype(jnp.bfloat16)
        else:
            acc_out[head] = mixed

    groups = [range(low, low + group) for low in range(0, heads, group)]
    found = {}
    for step in range(len(groups) + 3):
        if step < len(groups):
            for head in groups[step]:
                if head % 2 == 0:
                    expand(head // 2)
        if 0 <= step - 1 < len(groups):
            for head in groups[step - 1]:
                score(head)
        if 0 <= step - 2 < len(groups):
            for head in groups[step - 2]:
                found[head] = weigh(head)
        if 0 <= step - 3:
            for head in groups[step - 3]:
                mix(head, *found[head])


def key_table(views, rows, tok_dev):
    columns = []
    for half in range(2):
        for _, _, partner, across, slots in views:
            for k in slots:
                for turn in (0, 2):
                    place = [row - 2 * k * tok_dev for row in range(rows)]
                    columns += [(p, partner, turn, half, across) for p in place]
    return np.array(columns, np.int32).T


def attend(doc_lengths, queries, w_key, w_value, pieces, views, group, state, last):
    heads, rows, width = queries.shape
    first = state is None
    table = jnp.asarray(key_table(views, 16, rows))
    count = table.shape[1]
    vmem = pl.BlockSpec(memory_space=pltpu.VMEM)
    args = [queries, table, w_key, w_value, *pieces]
    if not first:
        args += list(state)
    args = [slow(doc_lengths), *[fast(a) for a in args]]
    if last:
        out_shape = jax.ShapeDtypeStruct((rows, heads * VD), jnp.bfloat16)
        out_specs = vmem
    else:
        out_shape = [pltpu.VMEM((heads, rows, VD), jnp.float32)] * 3
        out_specs = [vmem] * 3

    def kernel(*refs):
        attend_kernel(views, group, first, last, *refs)

    return pl.pallas_call(
        kernel,
        in_specs=[pl.BlockSpec(memory_space=pltpu.SMEM)] + [vmem] * (len(args) - 1),
        out_specs=out_specs,
        out_shape=out_shape,
        scratch_shapes=[
            pltpu.VMEM((count, KL), jnp.bfloat16),
            pltpu.VMEM((count, LANES), jnp.bfloat16),
            pltpu.VMEM((rows, count), jnp.float32),
            pltpu.VMEM((KL + LANES, count), jnp.bfloat16),
            pltpu.VMEM((heads * ND, count), jnp.bfloat16),
            pltpu.VMEM((count, heads * VD), jnp.bfloat16),
            pltpu.VMEM((heads, rows, count), jnp.float32),
            pltpu.VMEM((heads, rows, count), jnp.bfloat16),
        ],
        compiler_params=LARGE,
    )(*args)


def body(q_latent, q_gain, kv_cache, kv_gain, w_query, w_kv, doc_lengths):
    ctx_size, head_size = lax.axis_size("ctx"), lax.axis_size("head")
    chips, ys = ctx_size // 2, head_size // 2
    tok_dev = q_latent.shape[0] * head_size
    heads_here = w_query.shape[1] // (ND + RD)
    ctx, head = lax.axis_index("ctx"), lax.axis_index("head")
    vmem = pl.BlockSpec(memory_space=pltpu.VMEM)

    swap = [(n, n ^ 1) for n in range(ctx_size)]
    across_x = [(n, n ^ 1) for n in range(head_size)]

    def chip_shift(step):
        return [(2 * n + c, 2 * ((n + step) % chips) + c) for n in range(chips) for c in range(2)]

    apart = [
        ((2 * n + c) * head_size + h, (2 * n + c) * head_size + (h + 2 - 4 * c) % head_size)
        for n in range(chips)
        for c in range(2)
        for h in range(head_size)
    ]

    across_y = [(n, (n + ys) % head_size) for n in range(head_size)]

    size, q_width = q_latent.shape
    kv_width = kv_cache.shape[1]
    rows = pl.pallas_call(
        norm_kernel,
        out_shape=pltpu.VMEM((size, q_width + kv_width), jnp.bfloat16),
        compiler_params=SMALL,
    )(*[slow(a) for a in (q_latent, q_gain, kv_cache, kv_gain)])
    other = lax.ppermute(rows, "head", across_x)
    w_kv, rows = lax.optimization_barrier((w_kv, rows))
    w_key, w_value = pl.pallas_call(
        split_kernel,
        in_specs=[vmem],
        out_specs=[vmem] * 2,
        out_shape=[
            pltpu.VMEM((heads_here * ND, KL), jnp.bfloat16),
            pltpu.VMEM((KL, heads_here * VD), jnp.bfloat16),
        ],
        compiler_params=SMALL,
    )(fast(w_kv))
    both = pl.pallas_call(
        pair_kernel,
        in_specs=[vmem] * 3,
        out_specs=vmem,
        out_shape=pltpu.VMEM((size, 2 * rows.shape[1]), jnp.bfloat16),
        compiler_params=SMALL,
    )(fast(rows), fast(other), fast(w_key))
    opposite = lax.ppermute(both, "head", across_y)
    w_query, both = lax.optimization_barrier((w_query, both))
    w_query = pl.pallas_call(
        fetch_kernel,
        in_specs=[pl.BlockSpec(memory_space=pl.ANY)],
        out_specs=vmem,
        out_shape=pltpu.VMEM(w_query.shape, w_query.dtype),
        scratch_shapes=[pltpu.SemaphoreType.DMA],
        compiler_params=SMALL,
    )(slow(w_query))
    piece, q_set = pl.pallas_call(
        part_kernel,
        in_specs=[vmem] * 3,
        out_specs=[vmem] * 2,
        out_shape=[
            pltpu.VMEM((2 * size, 2 * kv_width), jnp.bfloat16),
            pltpu.VMEM((2 * size, 2 * q_width), jnp.bfloat16),
        ],
        compiler_params=SMALL,
    )(fast(both), fast(opposite), fast(w_query))
    coarse = [lax.ppermute(piece, "ctx", chip_shift(step)) for step in COARSE]
    set_shape = coarse[0].shape
    q_at = len(COARSE) * set_shape[1]
    coarse, bundle = pl.pallas_call(
        lambda *refs: bundle_kernel(len(COARSE), *refs),
        in_specs=[vmem] * (len(COARSE) + 1),
        out_specs=[vmem] * 2,
        out_shape=[
            pltpu.VMEM((len(COARSE) * set_shape[0], set_shape[1]), jnp.bfloat16),
            pltpu.VMEM((set_shape[0], q_at + q_set.shape[1]), jnp.bfloat16),
        ],
        compiler_params=SMALL,
    )(*[fast(a) for a in (*coarse, q_set)])
    later = lax.ppermute(coarse, "ctx", chip_shift(1))
    sooner = lax.ppermute(coarse, "ctx", chip_shift(-1))
    got = lax.ppermute(bundle, ("ctx", "head"), apart)
    coarse_swapped = lax.ppermute(coarse, "ctx", swap)

    (near,) = join([[later, sooner]])
    received = lax.ppermute(near, ("ctx", "head"), apart)
    near_swapped = lax.ppermute(near, "ctx", swap)
    got_swapped = lax.ppermute(got, "ctx", swap)

    queries = pl.pallas_call(
        lambda *refs: query_kernel(q_at, *refs),
        in_specs=[pl.BlockSpec(memory_space=pltpu.SMEM)] + [vmem] * 3,
        out_specs=vmem,
        out_shape=pltpu.VMEM((heads_here, tok_dev, 2 * LANES), jnp.bfloat16),
        scratch_shapes=[pltpu.VMEM((tok_dev, w_query.shape[0]), jnp.bfloat16)],
        compiler_params=SMALL,
    )(slow(doc_lengths), fast(q_set), fast(got), fast(w_query))

    def attend_to(pieces, views, group, state, last=False):
        return attend(doc_lengths, queries, w_key, w_value, pieces, views, group, state, last)

    near_slots = [*[k + 1 for k in COARSE], *[k - 1 for k in COARSE]]
    views = [(0, 0, 0, 0, COARSE), (1, 0, 0, 0, near_slots)]
    views += [(2, 0, 1, 0, COARSE), (3, 0, 1, 0, near_slots)]
    for partner in range(2):
        for n, k in enumerate(COARSE):
            views.append((4 + partner, n * set_shape[1], partner, 1, [k]))
    pieces = [coarse, near, coarse_swapped, near_swapped, got, got_swapped]
    state = attend_to(pieces, views, 2, None)
    received, state = lax.optimization_barrier((received, state))
    swapped = lax.ppermute(received, "ctx", swap)
    state = attend_to([received], [(0, 0, 0, 1, near_slots)], 2, state)
    return attend_to([swapped], [(0, 0, 1, 1, near_slots)], 2, state, last=True)


def solution(mesh):
    placed = (
        P(("ctx", "head"), None),
        P(),
        P(("ctx", "head"), None),
        P(),
        P(None, "head"),
        P(None, "head"),
        P(),
    )
    return jax.shard_map(
        body, mesh=mesh, in_specs=placed, out_specs=P("ctx", "head"), check_vma=False
    )
```

```python
import math

import jax
import jax.numpy as jnp
import numpy as np
from jax import lax
from jax.experimental import pallas as pl
from jax.experimental.pallas import tpu as pltpu
from jax.sharding import PartitionSpec as P

KL = 512
RD = 64
ND = 128
VD = 128
LANES = 128
EPSILON = 1e-06
MASKED = -1e30
FLOOR = -1e29
COARSE = (4, 1, 7)
SCORE_SCALE = math.log2(math.e) / math.sqrt(ND + RD)


SMALL = pltpu.CompilerParams(vmem_limit_bytes=12 * 2**20)
LARGE = pltpu.CompilerParams(vmem_limit_bytes=28 * 2**20)


def fast(array):
    return pltpu.with_memory_space_constraint(array, pltpu.VMEM)


def slow(array):
    return pltpu.with_memory_space_constraint(array, pltpu.HBM)


def here():
    ctx, head = lax.axis_index("ctx"), lax.axis_index("head")
    return ctx // 2, lax.rem(ctx, 2), head // 2, lax.rem(head, 2)


def scaled(values, gain):
    mean = jnp.mean(values * values, axis=-1, keepdims=True)
    return values * lax.rsqrt(mean + EPSILON) * gain


def norm_kernel(q_ref, q_gain_ref, kv_ref, kv_gain_ref, out_ref):
    latent = kv_ref[:, :KL].astype(jnp.float32)
    out_ref[:, :KL] = scaled(latent, kv_gain_ref[...][None, :]).astype(jnp.bfloat16)
    rows = q_ref[...].astype(jnp.float32)
    q_end = KL + rows.shape[1]
    out_ref[:, KL:q_end] = scaled(rows, q_gain_ref[...][None, :]).astype(jnp.bfloat16)
    out_ref[:, q_end:] = kv_ref[:, KL:]


def split_kernel(w_ref, key_ref, value_ref):
    for head in range(key_ref.shape[0] // ND):
        at = head * (ND + VD)
        key_ref[head * ND : (head + 1) * ND, :] = w_ref[:, at : at + ND].T
        value_ref[:, head * VD : (head + 1) * VD] = w_ref[:, at + ND : at + ND + VD]


def fetch_kernel(from_ref, to_ref, arrived):
    pltpu.async_copy(from_ref, to_ref, arrived).wait()


def pair_kernel(own_ref, other_ref, ready_ref, kv_ref, q_ref):
    q_end = own_ref.shape[1] - RD
    q_size = q_end - KL
    for n, ref in enumerate((own_ref, other_ref)):
        kv_ref[:, n * KL : (n + 1) * KL] = ref[:, :KL]
        q_ref[:, n * q_size : (n + 1) * q_size] = ref[:, KL:q_end]
    kv_ref[:, 2 * KL :] = jnp.concatenate([own_ref[:, q_end:], other_ref[:, q_end:]], axis=1)


def bundle_kernel(coarse_ref, q_own_ref, q_got_ref, q_ref, bundle_ref):
    size, width = q_ref.shape[0], coarse_ref.shape[1]
    n_parts = coarse_ref.shape[0] // size
    for n in range(n_parts):
        bundle_ref[:, n * width : (n + 1) * width] = coarse_ref[n * size : (n + 1) * size, :]
    for n, ref in enumerate((q_own_ref, q_got_ref)):
        rows = slice(n * ref.shape[0], (n + 1) * ref.shape[0])
        q_ref[rows, :] = ref[...]
        bundle_ref[rows, n_parts * width :] = ref[...]


def join_kernel(sizes, n_after, *refs):
    outs = refs[len(refs) - len(sizes) :]
    at = 0
    for size, out_ref in zip(sizes, outs):
        row = 0
        for ref in refs[at : at + size]:
            out_ref[row : row + ref.shape[0], :] = ref[...]
            row += ref.shape[0]
        at += size


def join(groups, after=()):
    sizes = [len(g) for g in groups]
    shapes = [
        pltpu.VMEM((sum(a.shape[0] for a in g), g[0].shape[1]), g[0].dtype)
        for g in groups
    ]
    arrays = [a for g in groups for a in g]
    vmem = pl.BlockSpec(memory_space=pltpu.VMEM)

    def kernel(*refs):
        join_kernel(sizes, len(after), *refs)

    return pl.pallas_call(
        kernel,
        in_specs=[vmem] * (len(arrays) + len(after)),
        out_specs=[vmem] * len(groups),
        out_shape=shapes,
        compiler_params=SMALL,
    )(*[fast(a) for a in (*arrays, *after)])


def document_start(position, lengths):
    start, end = jnp.zeros_like(position), 0
    for doc in range(lengths.shape[0]):
        end = end + lengths[doc]
        start = jnp.where(position >= end, end, start)
    return start


def query_kernel(q_at, lengths, own, got, w_ref, out_ref, rows_ref):
    chip, core, y, xh = here()
    width = rows_ref.shape[1]
    for base, ref, lane_at in ((y, own, 0), (y + jnp.where(core == 0, 3, 1), got, q_at)):
        for n in range(4):
            turn, half = n // 2, n % 2
            place = lax.rem(base + 2 * turn, 4) * 32 + lax.rem(xh + half, 2) * 16
            at = pl.multiple_of(place, 16)
            lanes = slice(lane_at + half * width, lane_at + (half + 1) * width)
            rows = ref[16 * turn : 16 * turn + 16, lanes]
            rows_ref[pl.ds(at, 16), :] = rows

    shape = (rows_ref.shape[0], LANES)
    lane = lax.broadcasted_iota(jnp.int32, shape, 1)
    position = (2 * chip + core) * shape[0] + lax.broadcasted_iota(jnp.int32, shape, 0)
    offset = (position - document_start(position, lengths)).astype(jnp.float32)
    freq_index = lax.rem(lane, RD // 2).astype(jnp.float32)
    angles = offset * jnp.exp(freq_index * (-2.0 * math.log(10000.0) / RD))
    cosine = jnp.where(lane < RD, jnp.cos(angles), 0.0)
    sine = jnp.sin(angles)
    sine = jnp.where(lane < RD // 2, -sine, jnp.where(lane < RD, sine, 0.0))

    def rotated(rope):
        turned = jnp.where(
            lane < RD // 2, pltpu.roll(rope, LANES - RD // 2, 1), pltpu.roll(rope, RD // 2, 1)
        )
        return rope * cosine + turned * sine

    pair_width = 2 * (ND + RD)
    for pair in range(w_ref.shape[1] // pair_width):
        w = w_ref[:, pair * pair_width : (pair + 1) * pair_width]
        made = jnp.dot(rows_ref[...], w, preferred_element_type=jnp.float32)
        out_ref[2 * pair, :, :ND] = made[:, :ND].astype(jnp.bfloat16)
        out_ref[2 * pair, :, ND:] = rotated(made[:, ND : ND + LANES]).astype(jnp.bfloat16)
        second = ND + RD
        out_ref[2 * pair + 1, :, :ND] = made[:, second : second + ND].astype(jnp.bfloat16)
        rope = pltpu.roll(made[:, second + RD : second + RD + LANES], RD, 1)
        out_ref[2 * pair + 1, :, ND:] = rotated(rope).astype(jnp.bfloat16)


def attend_kernel(views, group, first, last, *refs):
    lengths, q_ref, table_ref, w_key_ref, w_value_ref = refs[:5]
    at = 5 + 1 + max(view[0] for view in views)
    pieces = refs[5:at]
    if not first:
        max_in, sum_in, acc_in = refs[at : at + 3]
        at += 3
    if last:
        (out_ref,) = refs[at : at + 1]
        at += 1
    else:
        max_out, sum_out, acc_out = refs[at : at + 3]
        at += 3
    rows_ref, rope_ref, bias_ref, turned_ref, key_ref, value_ref, score_ref, weight_ref = refs[at : at + 8]
    if last:
        made_ref, gone = refs[at + 8 :]
    heads = q_ref.shape[0]
    tok_dev, n_keys = bias_ref.shape

    row = 0
    for piece, lane_at, *_ in views:
        ref = pieces[piece]
        size = ref.shape[0]
        rope = ref[:, lane_at + 2 * KL : lane_at + 2 * (KL + RD)]
        turned = jnp.concatenate([rope[:, RD:], rope[:, :RD]], axis=1)
        for half in range(2):
            to = slice(row + half * (n_keys // 2), row + half * (n_keys // 2) + size)
            rows_ref[to, :] = ref[:, lane_at + half * KL : lane_at + (half + 1) * KL]
            rope_ref[to, :] = turned if half else rope
        row += size

    chip, core, y, xh = here()
    query_pos = (2 * chip + core) * tok_dev + lax.broadcasted_iota(jnp.int32, (tok_dev, 1), 0)
    query_start = document_start(query_pos, lengths)
    place, partner, turn, half, across = [table_ref[n : n + 1, :] for n in range(5)]
    holder = lax.rem(core + partner, 2)
    ys = lax.rem(y + turn + across * (3 - 2 * holder), 4)
    xs = lax.rem(xh + half, 2)
    key_pos = place + (2 * chip + holder) * tok_dev + ys * 32 + xs * 16
    allowed = (key_pos <= query_pos) & (key_pos >= query_start)
    bias_ref[...] = jnp.where(allowed, 0.0, MASKED)

    turned_ref[:KL, :] = rows_ref[...].T
    turned_ref[KL:, :] = rope_ref[...].T

    def expand(pair):
        some = slice(pair * 2 * ND, (pair + 1) * 2 * ND)
        keys = jnp.dot(w_key_ref[some, :], turned_ref[:KL, :], preferred_element_type=jnp.float32)
        key_ref[some, :] = keys.astype(jnp.bfloat16)
        values = jnp.dot(rows_ref[...], w_value_ref[:, some], preferred_element_type=jnp.float32)
        value_ref[:, some] = values.astype(jnp.bfloat16)

    def score(head):
        keys = [key_ref[head * ND : (head + 1) * ND, :], turned_ref[KL:, :]]
        keys = jnp.concatenate(keys, axis=0)
        scores = jnp.dot(q_ref[head], keys, preferred_element_type=jnp.float32)
        score_ref[head] = scores * SCORE_SCALE + bias_ref[...]

    def weigh(head):
        scores = score_ref[head]
        top = jnp.broadcast_to(jnp.max(scores, axis=1, keepdims=True), (tok_dev, LANES))
        old_max = FLOOR if first else max_in[head]
        new_max = jnp.maximum(top, old_max)
        weights = jnp.exp2(scores - jnp.concatenate([new_max] * (n_keys // LANES), axis=1))
        total = jnp.broadcast_to(jnp.sum(weights, axis=1, keepdims=True), (tok_dev, LANES))
        weight_ref[head] = weights.astype(jnp.bfloat16)
        if not last:
            max_out[head] = new_max
        if first:
            sum_out[head] = total
            return total, None
        faded = jnp.exp2(old_max - new_max)
        total = total + faded * sum_in[head]
        if not last:
            sum_out[head] = total
        return total, faded

    def mix(head, total, faded):
        values = value_ref[:, head * VD : (head + 1) * VD]
        mixed = jnp.dot(weight_ref[head], values, preferred_element_type=jnp.float32)
        if not first:
            mixed = mixed + faded * acc_in[head]
        if last:
            made_ref[:, head * VD : (head + 1) * VD] = (mixed * (1.0 / total)).astype(jnp.bfloat16)
            if head % 2 == 1:
                copies[head // 2].start()
        else:
            acc_out[head] = mixed

    copies = []
    for pair in range(heads // 2 if last else 0):
        some = slice(pair * 2 * VD, (pair + 1) * 2 * VD)
        copy = pltpu.make_async_copy(made_ref.at[:, some], out_ref.at[:, some], gone.at[pair])
        copies.append(copy)
    groups = [range(low, low + group) for low in range(0, heads, group)]
    found = {}
    for step in range(len(groups) + 3):
        if step < len(groups):
            for head in groups[step]:
                if head % 2 == 0:
                    expand(head // 2)
        if 0 <= step - 1 < len(groups):
            for head in groups[step - 1]:
                score(head)
        if 0 <= step - 2 < len(groups):
            for head in groups[step - 2]:
                found[head] = weigh(head)
        if 0 <= step - 3:
            for head in groups[step - 3]:
                mix(head, *found[head])
    for copy in copies:
        copy.wait()


def key_table(views, rows, tok_dev):
    columns = []
    for half in range(2):
        for _, _, partner, across, slots in views:
            for k in slots:
                for turn in (0, 2):
                    place = [row - 2 * k * tok_dev for row in range(rows)]
                    columns += [(p, partner, turn, half, across) for p in place]
    return np.array(columns, np.int32).T


def attend(doc_lengths, queries, w_key, w_value, pieces, views, group, state, last):
    heads, rows, width = queries.shape
    first = state is None
    table = jnp.asarray(key_table(views, 16, rows))
    count = table.shape[1]
    vmem = pl.BlockSpec(memory_space=pltpu.VMEM)
    args = [queries, table, w_key, w_value, *pieces]
    if not first:
        args += list(state)
    args = [slow(doc_lengths), *[fast(a) for a in args]]
    if last:
        out_shape = jax.ShapeDtypeStruct((rows, heads * VD), jnp.bfloat16)
        out_specs = pl.BlockSpec(memory_space=pl.ANY)
        leaving = [
            pltpu.VMEM((rows, heads * VD), jnp.bfloat16),
            pltpu.SemaphoreType.DMA((heads // 2,)),
        ]
    else:
        leaving = []
        out_shape = [pltpu.VMEM((heads, rows, VD), jnp.float32)] * 3
        out_specs = [vmem] * 3

    def kernel(*refs):
        attend_kernel(views, group, first, last, *refs)

    return pl.pallas_call(
        kernel,
        in_specs=[pl.BlockSpec(memory_space=pltpu.SMEM)] + [vmem] * (len(args) - 1),
        out_specs=out_specs,
        out_shape=out_shape,
        scratch_shapes=[
            pltpu.VMEM((count, KL), jnp.bfloat16),
            pltpu.VMEM((count, LANES), jnp.bfloat16),
            pltpu.VMEM((rows, count), jnp.float32),
            pltpu.VMEM((KL + LANES, count), jnp.bfloat16),
            pltpu.VMEM((heads * ND, count), jnp.bfloat16),
            pltpu.VMEM((count, heads * VD), jnp.bfloat16),
            pltpu.VMEM((heads, rows, count), jnp.float32),
            pltpu.VMEM((heads, rows, count), jnp.bfloat16),
            *leaving,
        ],
        compiler_params=LARGE,
    )(*args)


def body(q_latent, q_gain, kv_cache, kv_gain, w_query, w_kv, doc_lengths):
    ctx_size, head_size = lax.axis_size("ctx"), lax.axis_size("head")
    chips, ys = ctx_size // 2, head_size // 2
    tok_dev = q_latent.shape[0] * head_size
    heads_here = w_query.shape[1] // (ND + RD)
    ctx, head = lax.axis_index("ctx"), lax.axis_index("head")
    vmem = pl.BlockSpec(memory_space=pltpu.VMEM)

    swap = [(n, n ^ 1) for n in range(ctx_size)]
    across_x = [(n, n ^ 1) for n in range(head_size)]

    def chip_shift(step):
        return [(2 * n + c, 2 * ((n + step) % chips) + c) for n in range(chips) for c in range(2)]

    apart = [
        ((2 * n + c) * head_size + h, (2 * n + c) * head_size + (h + 2 - 4 * c) % head_size)
        for n in range(chips)
        for c in range(2)
        for h in range(head_size)
    ]

    across_y = [(n, (n + ys) % head_size) for n in range(head_size)]

    size, q_width = q_latent.shape
    kv_width = kv_cache.shape[1]
    rows = pl.pallas_call(
        norm_kernel,
        out_shape=pltpu.VMEM((size, q_width + kv_width), jnp.bfloat16),
        compiler_params=SMALL,
    )(*[slow(a) for a in (q_latent, q_gain, kv_cache, kv_gain)])
    other = lax.ppermute(rows, "head", across_x)
    w_kv, rows = lax.optimization_barrier((w_kv, rows))
    w_key, w_value = pl.pallas_call(
        split_kernel,
        in_specs=[vmem],
        out_specs=[vmem] * 2,
        out_shape=[
            pltpu.VMEM((heads_here * ND, KL), jnp.bfloat16),
            pltpu.VMEM((KL, heads_here * VD), jnp.bfloat16),
        ],
        compiler_params=SMALL,
    )(fast(w_kv))
    piece, q_pair = pl.pallas_call(
        pair_kernel,
        in_specs=[vmem] * 3,
        out_specs=[vmem] * 2,
        out_shape=[
            pltpu.VMEM((size, 2 * kv_width), jnp.bfloat16),
            pltpu.VMEM((size, 2 * q_width), jnp.bfloat16),
        ],
        compiler_params=SMALL,
    )(fast(rows), fast(other), fast(w_key))
    opposite = lax.ppermute(piece, "head", across_y)
    (piece,) = join([[piece, opposite]])
    w_query, piece = lax.optimization_barrier((w_query, piece))
    w_query = pl.pallas_call(
        fetch_kernel,
        in_specs=[pl.BlockSpec(memory_space=pl.ANY)],
        out_specs=vmem,
        out_shape=pltpu.VMEM(w_query.shape, w_query.dtype),
        scratch_shapes=[pltpu.SemaphoreType.DMA],
        compiler_params=SMALL,
    )(slow(w_query))
    q_opposite = lax.ppermute(q_pair, "head", across_y)
    coarse = [lax.ppermute(piece, "ctx", chip_shift(step)) for step in COARSE]

    set_shape = coarse[0].shape
    q_at = len(COARSE) * set_shape[1]
    (coarse,) = join([coarse], after=[w_query])
    q_set, bundle = pl.pallas_call(
        bundle_kernel,
        in_specs=[vmem] * 3,
        out_specs=[vmem] * 2,
        out_shape=[
            pltpu.VMEM((set_shape[0], q_pair.shape[1]), jnp.bfloat16),
            pltpu.VMEM((set_shape[0], q_at + q_pair.shape[1]), jnp.bfloat16),
        ],
        compiler_params=SMALL,
    )(*[fast(a) for a in (coarse, q_pair, q_opposite)])
    coarse, bundle = lax.optimization_barrier((coarse, bundle))
    later = lax.ppermute(coarse, "ctx", chip_shift(1))
    sooner = lax.ppermute(coarse, "ctx", chip_shift(-1))
    got = lax.ppermute(bundle, ("ctx", "head"), apart)
    coarse_swapped = lax.ppermute(coarse, "ctx", swap)

    queries = pl.pallas_call(
        lambda *refs: query_kernel(q_at, *refs),
        in_specs=[pl.BlockSpec(memory_space=pltpu.SMEM)] + [vmem] * 3,
        out_specs=vmem,
        out_shape=pltpu.VMEM((heads_here, tok_dev, 2 * LANES), jnp.bfloat16),
        scratch_shapes=[pltpu.VMEM((tok_dev, w_query.shape[0]), jnp.bfloat16)],
        compiler_params=SMALL,
    )(slow(doc_lengths), fast(q_set), fast(got), fast(w_query))

    (near,) = join([[later, sooner]], after=[got])
    received = lax.ppermute(near, ("ctx", "head"), apart)
    near_swapped = lax.ppermute(near, "ctx", swap)
    got_swapped = lax.ppermute(got, "ctx", swap)

    def attend_to(pieces, views, group, state, last=False):
        return attend(doc_lengths, queries, w_key, w_value, pieces, views, group, state, last)

    near_slots = [*[k + 1 for k in COARSE], *[k - 1 for k in COARSE]]
    views = [(0, 0, 0, 0, COARSE), (1, 0, 0, 0, near_slots)]
    views += [(2, 0, 1, 0, COARSE), (3, 0, 1, 0, near_slots)]
    pieces = [coarse, near, coarse_swapped, near_swapped]
    state = attend_to(pieces, views, 2, None)
    received, got_swapped, state = lax.optimization_barrier((received, got_swapped, state))
    swapped = lax.ppermute(received, "ctx", swap)
    views = []
    for partner in range(2):
        for n, k in enumerate(COARSE):
            views.append((partner, n * set_shape[1], partner, 1, [k]))
    state = attend_to([got, got_swapped], views, 2, state)
    views = [(n, 0, n, 1, near_slots) for n in range(2)]
    return attend_to([received, swapped], views, 2, state, last=True)


def solution(mesh):
    placed = (
        P(("ctx", "head"), None),
        P(),
        P(("ctx", "head"), None),
        P(),
        P(None, "head"),
        P(None, "head"),
        P(),
    )
    return jax.shard_map(
        body, mesh=mesh, in_specs=placed, out_specs=P("ctx", "head"), check_vma=False
    )
```
